256 devices in a mesh: ctx: 64 (over z, x_lo, y), head: 4 (over x_hi, core).
Axes of the slice: x: 4 (x_hi: 2, x_lo: 2; x = x_hi * 2 + x_lo), y: 4, z: 8, core: 2. Of those that a mesh axis runs over, the one named last changes fastest.
Arguments:
- qkv: bfloat16 [3, 32768, 5120], P(None, 'ctx', 'head'), may hold values from -8 to 8
- step_size: float32 [32768, 8], P('ctx', 'head'), may hold values from 0.01 to 0.1
- fast_in: bfloat16 [8, 640, 1024], P('head'), may hold values from -1 to 1
- fast_out: bfloat16 [8, 512, 640], P('head'), may hold values from -1 to 1
Outputs:
- mixed: bfloat16 [32768, 5120], P('ctx', 'head')
The draws below stay inside these ranges and needn't reach their ends.
All inputs are finite; a program needn't handle non-finite values.
Results may differ from the reference program's by a relative error of at most 0.0087.
Values may be sent and summed in bfloat16 or wider, within the bound.
A program may use at most 128 MiB of HBM per device.

```python
import math
import jax
import jax.numpy as jnp
from jax import lax

D = 5120
ADIM = 128
FW_HEADS = 8
FH = 512
HD = 640
TOK_DEV = 512
TOKENS = 32768
WINDOW = 1024


def base_values(key_base, full_shape):
    return jnp.clip(jax.random.normal(key_base, full_shape, jnp.float32), -2.5, 2.5)


def column_scaled(key, full_shape, fan_in):
    key_base, key_scale = jax.random.split(key)
    base_draw = base_values(key_base, full_shape)
    scales = jnp.exp(jax.random.uniform(key_scale, (full_shape[0], 1, full_shape[2]), jnp.float32, math.log(0.3), math.log(3.0)))
    return base_draw * scales * fan_in ** (-0.5)


def draw_fast_in(key, part):
    key_base, key_scale, key_jitter = jax.random.split(jax.random.fold_in(key, 11), 3)
    full_shape = (FW_HEADS, HD, 2 * FH)
    base_draw = base_values(key_base, full_shape)
    gate_scale = jnp.exp(jax.random.uniform(key_scale, (FW_HEADS, 1, FH), jnp.float32, math.log(0.3), math.log(3.0)))
    jitter = jnp.exp(jax.random.uniform(key_jitter, (FW_HEADS, 1, FH), jnp.float32, math.log(0.6), math.log(0.9)))
    up_scale = jitter / gate_scale
    scales = jnp.concatenate([gate_scale, up_scale], axis=2)
    return (base_draw * scales * HD ** (-0.5)).astype(jnp.bfloat16)


def draw_fast_out(key, part):
    return column_scaled(jax.random.fold_in(key, 13), (FW_HEADS, FH, HD), FH).astype(jnp.bfloat16)


def draw_qkv(key, part):
    key_base = jax.random.fold_in(jax.random.fold_in(key, 7), 0)
    full_shape = (3, TOKENS, D)
    base_draw = jnp.clip(1.5 * jax.random.normal(key_base, full_shape, jnp.float32), -8.0, 8.0)
    return base_draw.astype(jnp.bfloat16)


def block_levels(stream_key, extent, pieces, least, largest):
    level = 1.0
    for axis_at, parts in pieces:
        draws = jax.random.uniform(jax.random.fold_in(jax.random.fold_in(stream_key, 6), axis_at), (parts,), jnp.float32, least / len(pieces), largest / len(pieces))
        level = level * jnp.repeat(jnp.exp(draws), extent[axis_at] // parts).reshape((-1,) + (1,) * (len(extent) - 1 - axis_at))
    return level


def setup_inputs(seed: int = 0) -> dict:
    streams_of = jax.random.split(jax.random.key(seed), 5)
    return {
        "qkv": draw_qkv(jax.random.fold_in(streams_of[4], 71), 0),
        "step_size": jnp.clip(jnp.exp(math.log(0.1) - 2.3025851 * jax.random.uniform(streams_of[1], (TOKENS, FW_HEADS), jnp.float32) ** block_levels(streams_of[1], (TOKENS, FW_HEADS), ((0, 64), (1, 4)), -0.2, 0.2)), 0.01, 0.1),
        "fast_in": draw_fast_in(jax.random.fold_in(streams_of[4], 71), 0),
        "fast_out": draw_fast_out(jax.random.fold_in(streams_of[4], 71), 0),
    }


EPS = 1e-06

def silu_parts(gate_part):
    sigmoid_part = jax.nn.sigmoid(gate_part)
    return (gate_part * sigmoid_part, sigmoid_part * (1.0 + gate_part * (1.0 - sigmoid_part)))

def renorm(weight, update, norm_axis):
    old_value = weight.astype(jnp.float32)
    moved_value = old_value + update
    old_norm = jnp.sqrt(lax.optimization_barrier(jnp.sum(old_value * old_value, axis=norm_axis, keepdims=True)))
    new_norm = jnp.sqrt(lax.optimization_barrier(jnp.sum(moved_value * moved_value, axis=norm_axis, keepdims=True)))
    return (moved_value * (old_norm / (new_norm + EPS))).astype(jnp.bfloat16)

def fast_head(inputs):
    queries, key_rows, values, rates, w_in, w_out = inputs
    projected = jnp.dot(key_rows, w_in, preferred_element_type=jnp.float32)
    gate_part = projected[:, :FH]
    up_part = projected[:, FH:]
    activated, slope_part = silu_parts(gate_part)
    hidden = (activated * up_part).astype(jnp.bfloat16)
    scaled = (rates[:, None] * values.astype(jnp.float32)).astype(jnp.bfloat16)
    back_part = jnp.dot(scaled, w_out.T, preferred_element_type=jnp.float32)
    pre_grad = jnp.concatenate([back_part * up_part * slope_part, back_part * activated], axis=1).astype(jnp.bfloat16)
    grad_in = jnp.dot(key_rows.T, pre_grad, preferred_element_type=jnp.float32)
    grad_out = jnp.dot(hidden.T, scaled, preferred_element_type=jnp.float32)
    factor = TOKENS ** (-0.5)
    new_in = renorm(w_in, grad_in * factor, 0)
    new_out = renorm(w_out, grad_out * factor, 0)
    query_proj = jnp.dot(queries, new_in, preferred_element_type=jnp.float32)
    query_act, unused_slope = silu_parts(query_proj[:, :FH])
    query_hidden = (query_act * query_proj[:, FH:]).astype(jnp.bfloat16)
    return jnp.dot(query_hidden, new_out, preferred_element_type=jnp.float32)

def band_attention(queries, key_rows, values):
    head_count = D // ADIM
    block_rows = TOK_DEV
    block_count = TOKENS // TOK_DEV
    padding = jnp.zeros((WINDOW, D), jnp.bfloat16)
    key_padded = jnp.concatenate([padding, key_rows], axis=0)
    value_padded = jnp.concatenate([padding, values], axis=0)
    row_pos = lax.broadcasted_iota(jnp.int32, (block_rows, block_rows + WINDOW), 0)
    col_pos = lax.broadcasted_iota(jnp.int32, (block_rows, block_rows + WINDOW), 1)

    def one_block(block_index):
        row_start = (block_index * block_rows).astype(jnp.int32)
        query_block = lax.dynamic_slice_in_dim(queries, row_start, block_rows, 0).reshape(block_rows, head_count, ADIM).astype(jnp.float32)
        key_block = lax.dynamic_slice_in_dim(key_padded, row_start, block_rows + WINDOW, 0).reshape(block_rows + WINDOW, head_count, ADIM).astype(jnp.float32)
        value_block = lax.dynamic_slice_in_dim(value_padded, row_start, block_rows + WINDOW, 0).reshape(block_rows + WINDOW, head_count, ADIM).astype(jnp.float32)
        scores = jnp.einsum('qhd,khd->hqk', query_block, key_block) * ADIM ** (-0.5)
        allowed = (col_pos > row_pos) & (col_pos <= row_pos + WINDOW) & (col_pos + row_start >= WINDOW)
        scores = jnp.where(allowed[None], scores, -1e+30)
        row_max = lax.optimization_barrier(jnp.max(scores, axis=-1, keepdims=True))
        weights = jnp.where(allowed[None], jnp.exp(scores - row_max), 0.0)
        row_total = lax.optimization_barrier(jnp.sum(weights, axis=-1, keepdims=True))
        probs_bf = (weights / row_total).astype(jnp.bfloat16)
        result = jnp.einsum('hqk,khd->qhd', probs_bf.astype(jnp.float32), value_block)
        return result.reshape(block_rows, D)
    blocks = lax.map(one_block, jnp.arange(block_count, dtype=jnp.int32))
    return blocks.reshape(TOKENS, D)

def reference(qkv, step_size, fast_in, fast_out):
    queries = qkv[0]
    key_rows = qkv[1]
    values = qkv[2]
    attended = band_attention(queries, key_rows, values)

    def by_head(array):
        return array.reshape(TOKENS, FW_HEADS, HD).transpose(1, 0, 2)
    applied = lax.map(fast_head, (by_head(queries), by_head(key_rows), by_head(values), step_size.T, fast_in, fast_out))
    applied = applied.transpose(1, 0, 2).reshape(TOKENS, D)
    return (attended + applied).astype(jnp.bfloat16)
```

```python
import functools

import jax
import jax.numpy as jnp
from jax import lax
from jax.experimental import pallas as pl
from jax.experimental.pallas import tpu as pltpu
from jax.sharding import PartitionSpec as P

ADIM = 128
FH = 512
HD = 640
TOK = 512
COLS = 1280
EPS = 1e-06
FACTOR = 32768.0 ** -0.5
SCALE = 1.4426950408889634 * ADIM ** -0.5
STRAND = 256
PLUS = (0, 1, 2)
MINUS = (3, 4)
BF = jnp.bfloat16
F32 = jnp.float32
MESH = pl.DeviceIdType.MESH
MESSAGES = 160


def nt(a, b):
    return lax.dot_general(a, b, (((1,), (1,)), ((), ())), preferred_element_type=F32)


def nn(a, b):
    return jnp.dot(a, b, preferred_element_type=F32)


def mult(index, of):
    return pl.multiple_of(index, of)


def kernel(
    qkv, step, w_in, w_out, out,
    kv, q, wi, wo, g, mi, mo, r1, r0, xb, x1, t1, u0, u1, ys, yr, pst, sst, att,
    local_sem, ss, rs,
):
    c = lax.axis_index("ctx")
    head = lax.axis_index("head")
    y = lax.rem(c, 4)
    x = lax.rem(c // 4, 2)
    z = c // 8
    other = 1 - x
    s_own = 2 * z + x

    def at(zz, xx, yy):
        return (8 * lax.rem(zz + 16, 8) + 4 * xx + lax.rem(yy + 8, 4), head)

    y_dev = {j: at(z, x, y + j) for j in (-1, 1, 2, 3)}
    z_dev = (at(z + 1, x, y), at(z - 1, x, y))
    x_dev = at(z, other, y)
    next_dev = (lax.rem(c + 4, 64), head)
    prev_dev = (lax.rem(c + 60, 64), head)

    used = [0]
    sent = []

    def message(size_ref, always=True):
        index = used[0]
        used[0] += 1
        if always:
            sent.append((index, size_ref))
        return index

    def copy(index, src, dst, device):
        return pltpu.make_async_remote_copy(
            src_ref=src, dst_ref=dst, send_sem=ss.at[index], recv_sem=rs.at[index],
            device_id=device, device_id_type=MESH,
        )

    def landed(index, ref):
        copy(index, ref, ref, x_dev).wait_recv()

    barrier = pltpu.get_barrier_semaphore()
    for device in (y_dev[1], y_dev[2], y_dev[3], *z_dev, x_dev, next_dev, prev_dev):
        pl.semaphore_signal(barrier, inc=1, device_id=device, device_id_type=MESH)

    locals_ = []

    def fetch(src, dst):
        cp = pltpu.make_async_copy(src, dst, local_sem.at[len(locals_)])
        cp.start()
        locals_.append(cp)

    own_rows = pl.ds(2 * TOK, TOK)
    near_rows = pl.ds(TOK, TOK)
    far_rows = pl.ds(0, TOK)
    fetch(qkv.at[pl.ds(1, 2)], kv.at[:, own_rows])
    fetch(w_in, wi)
    fetch(w_out, wo)
    fetch(qkv.at[0], q)
    pl.semaphore_wait(barrier, 8)

    def cols(strand):
        return pl.ds(strand * STRAND, STRAND)

    def own(strand):
        return qkv.at[pl.ds(1, 2), :, cols(strand)]

    def near(strand):
        return kv.at[:, near_rows, cols(strand)]

    def far(strand):
        return kv.at[:, far_rows, cols(strand)]

    pid = {}
    for strand in PLUS:
        for name in ("near", "far", "c3", "c2"):
            pid[strand, name] = message(None, False)
    for strand in MINUS:
        for name in ("u1", "u2", "u3", "cfar", "cnear"):
            pid[strand, name] = message(None, False)

    def plus_start(strand):
        @pl.when(y < 3)
        def _():
            copy(pid[strand, "near"], own(strand), near(strand), y_dev[1]).start()

        @pl.when(y == 3)
        def _():
            copy(pid[strand, "c3"], own(strand), pst.at[strand, 0], next_dev).start()

    def plus_cross_near(strand):
        @pl.when(y == 3)
        def _():
            landed(pid[strand, "c3"], pst.at[strand, 0])
            copy(pid[strand, "near"], pst.at[strand, 0], near(strand), y_dev[1]).start()

    def plus_forward(strand):
        landed(pid[strand, "near"], near(strand))

        @pl.when(y < 3)
        def _():
            copy(pid[strand, "far"], near(strand), far(strand), y_dev[1]).start()

        @pl.when(y == 3)
        def _():
            copy(pid[strand, "c2"], near(strand), pst.at[strand, 1], next_dev).start()

    def plus_cross_far(strand):
        @pl.when(y == 3)
        def _():
            landed(pid[strand, "c2"], pst.at[strand, 1])
            copy(pid[strand, "far"], pst.at[strand, 1], far(strand), y_dev[1]).start()

    def plus_done(strand):
        landed(pid[strand, "far"], far(strand))

    def minus_start(strand):
        m = strand - MINUS[0]
        copy(pid[strand, "u1"], own(strand), sst.at[m, 0], y_dev[-1]).start()

    def minus_second(strand):
        m = strand - MINUS[0]
        landed(pid[strand, "u1"], sst.at[m, 0])

        @pl.when(y == 3)
        def _():
            copy(pid[strand, "u2"], sst.at[m, 0], far(strand), y_dev[-1]).start()

        @pl.when(y == 0)
        def _():
            copy(pid[strand, "u2"], sst.at[m, 0], far(strand), y_dev[-1]).start()

        @pl.when((y == 1) | (y == 2))
        def _():
            copy(pid[strand, "u2"], sst.at[m, 0], sst.at[m, 1], y_dev[-1]).start()

    def minus_third(strand):
        m = strand - MINUS[0]

        @pl.when(y >= 2)
        def _():
            landed(pid[strand, "u2"], far(strand))
            copy(pid[strand, "u3"], far(strand), near(strand), y_dev[-1]).start()

        @pl.when(y == 1)
        def _():
            landed(pid[strand, "u2"], sst.at[m, 1])
            copy(pid[strand, "u3"], sst.at[m, 1], sst.at[m, 2], y_dev[-1]).start()
            copy(pid[strand, "cfar"], sst.at[m, 1], far(strand), next_dev).start()

        @pl.when(y == 0)
        def _():
            landed(pid[strand, "u2"], sst.at[m, 1])
            copy(pid[strand, "u3"], sst.at[m, 1], near(strand), y_dev[-1]).start()
            copy(pid[strand, "cfar"], sst.at[m, 1], far(strand), next_dev).start()

    def minus_cross(strand):
        m = strand - MINUS[0]

        @pl.when(y == 0)
        def _():
            landed(pid[strand, "u3"], sst.at[m, 2])
            copy(pid[strand, "cnear"], sst.at[m, 2], near(strand), next_dev).start()

    def minus_done(strand):
        @pl.when(y > 0)
        def _():
            landed(pid[strand, "u3"], near(strand))

        @pl.when(y == 0)
        def _():
            landed(pid[strand, "cnear"], near(strand))

        @pl.when(y <= 1)
        def _():
            landed(pid[strand, "cfar"], far(strand))

    def halo_sends_done():
        for strand in PLUS:
            piece = near(strand)
            copy(pid[strand, "near"], piece, piece, x_dev).wait_send()
            copy(pid[strand, "far"], piece, piece, x_dev).wait_send()

            @pl.when(y == 3)
            def _():
                copy(pid[strand, "c3"], piece, piece, x_dev).wait_send()
                copy(pid[strand, "c2"], piece, piece, x_dev).wait_send()

        for strand in MINUS:
            piece = near(strand)
            for name in ("u1", "u2", "u3"):
                copy(pid[strand, name], piece, piece, x_dev).wait_send()

            @pl.when(y <= 1)
            def _():
                copy(pid[strand, "cfar"], piece, piece, x_dev).wait_send()

            @pl.when(y == 0)
            def _():
                copy(pid[strand, "cnear"], piece, piece, x_dev).wait_send()

    def gradients(h):
        hc = pl.ds(h * HD, HD)
        keys = kv[0, own_rows, hc]
        vals = kv[1, own_rows, hc]
        rate = step[:, h:h + 1]
        scaled = (rate * vals.astype(F32)).astype(BF)
        gate = nt(wi[h, 0:FH], keys)
        up = nt(wi[h, FH:2 * FH], keys)
        back = nt(wo[h], scaled)
        sig = jax.nn.sigmoid(gate)
        act = gate * sig
        hidden = (act * up).astype(BF)
        d_gate = (back * up * sig * (1.0 + gate * (1.0 - sig))).astype(BF)
        d_up = (back * act).astype(BF)
        g_gate = nn(d_gate, keys).astype(BF)
        for s in range(8):
            g[h, s, 0:64] = g_gate[64 * s:64 * s + 64]
        g_up = nn(d_up, keys).astype(BF)
        for s in range(8):
            g[h, 8 + s, 0:64] = g_up[64 * s:64 * s + 64]
        g_out = nn(hidden, scaled).astype(BF)
        for s in range(16):
            g[h, s, 64:96] = g_out[32 * s:32 * s + 32]

    def add(dst, src):
        dst[...] = (dst[...].astype(F32) + src[...].astype(F32)).astype(BF)

    def z_of(direction, distance):
        offset = distance if direction == 0 else -distance
        return lax.rem(z + offset + 8, 8)

    def chains(k):
        for direction in (0, 1):
            for half in (direction, 1 - direction):
                start = 0 if half == direction else 1
                if k >= start:
                    yield direction, half, k == start

    ring1 = {(d, h, k): message(r1.at[0, 0, 0]) for k in range(4) for d, h, _ in chains(k)}
    ring0 = {(d, h, k): message(r0.at[0, 0, 0]) for k in range(4) for d, h, _ in chains(k)}
    cross0 = [message(xb.at[0]) for _ in range(8)]
    cross1 = message(x1)

    def ring1_step(k):
        for direction, half, first in chains(k):
            part = g.at[1, 2 * z_of(direction, 4 - k) + half]
            if first:
                src = part
            else:
                src = r1.at[direction, half, k - 1]
                landed(ring1[direction, half, k - 1], src)
                add(src, part)
            copy(ring1[direction, half, k], src, r1.at[direction, half, k], z_dev[direction]).start()

    def ring1_end():
        for direction in (0, 1):
            for half in (0, 1):
                landed(ring1[direction, half, 3], r1.at[direction, half, 3])

        def total(half):
            return (
                g[1, 2 * z + half].astype(F32)
                + r1[0, half, 3].astype(F32)
                + r1[1, half, 3].astype(F32)
            )

        t1[...] = total(other).astype(BF)
        copy(cross1, t1, x1, x_dev).start()
        u1[...] = total(x)

    slots = [(0, 4), (0, 3), (1, 3), (0, 2), (1, 2), (0, 1), (1, 1), (0, 0)]
    slot_of = {pair: i for i, pair in enumerate(slots)}
    slot_of[1, 4] = 0

    def cross0_start():
        for i, (direction, distance) in enumerate(slots):
            copy(
                cross0[i], g.at[0, 2 * z_of(direction, distance) + other], xb.at[i], x_dev
            ).start()

    def cross0_add(i):
        landed(cross0[i], xb.at[i])
        direction, distance = slots[i]
        add(xb.at[i], g.at[0, 2 * z_of(direction, distance) + x])

    def ring0_step(k):
        for i in {0: (0,), 1: (1, 2), 2: (3, 4), 3: (5, 6)}[k]:
            cross0_add(i)
        for direction, half, first in chains(k):
            part = xb.at[slot_of[direction, 4 - k], pl.ds(48 * half, 48)]
            if first:
                src = part
            else:
                src = r0.at[direction, half, k - 1]
                landed(ring0[direction, half, k - 1], src)
                add(src, part)
            copy(ring0[direction, half, k], src, r0.at[direction, half, k], z_dev[direction]).start()

    def ring0_end():
        cross0_add(7)
        for half in (0, 1):
            rows = pl.ds(48 * half, 48)
            for direction in (0, 1):
                landed(ring0[direction, half, 3], r0.at[direction, half, 3])
            u0[rows] = (
                xb[7, rows].astype(F32) + r0[0, half, 3].astype(F32) + r0[1, half, 3].astype(F32)
            )

    y_sum = {j: message(ys.at[0]) for j in (1, 2, 3)}

    def y_reduce():
        landed(cross1, x1)
        u1[...] = u1[...] + x1[...].astype(F32)
        for p in range(4):
            ys[p, 0:16] = u0[16 * p:16 * p + 16].astype(BF)
            ys[p, 16:32] = u1[16 * p:16 * p + 16].astype(BF)
            source = u0 if p < 2 else u1
            first = 64 + 16 * (p % 2)
            ys[p, 32:48] = source[first:first + 16].astype(BF)
        for j in (1, 2, 3):
            copy(y_sum[j], ys.at[lax.rem(y + j, 4)], yr.at[j - 1], y_dev[j]).start()
        for j in (1, 2, 3):
            landed(y_sum[j], yr.at[j - 1])

    in_row = mult(64 * s_own + 16 * y, 16)
    out_head = y // 2
    out_row = mult(32 * s_own + 16 * lax.rem(y, 2), 16)

    def renorm():
        total = ys[y].astype(F32)
        for j in range(3):
            total = total + yr[j].astype(F32)
        for h in (0, 1):
            old = wi[h, pl.ds(in_row, 16)].astype(F32)
            moved = old + total[16 * h:16 * h + 16] * FACTOR
            old_norm = jnp.sqrt(jnp.sum(old * old, axis=1, keepdims=True))
            new_norm = jnp.sqrt(jnp.sum(moved * moved, axis=1, keepdims=True))
            mi[h, pl.ds(in_row, 16)] = (moved * (old_norm / (new_norm + EPS))).astype(BF)
        old = wo[out_head, pl.ds(out_row, 16)].astype(F32)
        mo[out_head, pl.ds(out_row, 16)] = (old + total[32:48] * FACTOR).astype(BF)

    sixteen = mi.at[0, pl.ds(0, 16)]
    y_all = {(j, i): message(sixteen) for j in (1, 2, 3) for i in range(3)}

    def y_gather():
        pieces = (
            mi.at[0, pl.ds(in_row, 16)],
            mi.at[1, pl.ds(in_row, 16)],
            mo.at[out_head, pl.ds(out_row, 16)],
        )
        for j in (1, 2, 3):
            for i, piece in enumerate(pieces):
                copy(y_all[j, i], piece, piece, y_dev[j]).start()
        for j in (1, 2, 3):
            yy = lax.rem(y - j + 4, 4)
            row = mult(64 * s_own + 16 * yy, 16)
            landed(y_all[j, 0], mi.at[0, pl.ds(row, 16)])
            landed(y_all[j, 1], mi.at[1, pl.ds(row, 16)])
            row = mult(32 * s_own + 16 * lax.rem(yy, 2), 16)
            landed(y_all[j, 2], mo.at[yy // 2, pl.ds(row, 16)])

    def chunk(h, zz, part=None, xx=None):
        rows = 128 if h == 1 else 64
        first = 128 * zz + (64 * (x if xx is None else xx) if h == 0 or xx is not None else 0)
        if xx is not None:
            rows = 64
        n_in, f_in = rows, first
        n_out, f_out = rows // 2, first // 2
        if part is not None:
            n_in, n_out = n_in // 2, n_out // 2
            f_in = f_in + part * n_in
            f_out = f_out + part * n_out
        return (
            mi.at[h, pl.ds(mult(f_in, 16), n_in)],
            mo.at[h, pl.ds(mult(f_out, 16), n_out)],
        )

    def pair_ids(h, part=None, xx=None):
        return tuple(message(ref) for ref in chunk(h, 0, part, xx))

    def push(ids, refs, device):
        for index, ref in zip(ids, refs):
            copy(index, ref, ref, device).start()

    def pushed(ids, refs):
        for index, ref in zip(ids, refs):
            landed(index, ref)

    gather = {
        (h, j, d): pair_ids(h, d if j == 4 else None)
        for h in (0, 1) for j in (1, 2, 3, 4) for d in (0, 1)
    }
    share0 = [pair_ids(0) for _ in range(8)]
    share1 = pair_ids(1, None, x)

    def gather_send(h, j):
        for d in (0, 1):
            part = d if j == 4 else None
            push(gather[h, j, d], chunk(h, z_of(1 - d, j - 1), part), z_dev[d])

    def gather_wait(h, j):
        for d in (0, 1):
            part = d if j == 4 else None
            pushed(gather[h, j, d], chunk(h, z_of(1 - d, j), part))

    share_order = [(0, 0)] + [(d, j) for j in (1, 2, 3) for d in (0, 1)] + [(0, 4)]

    def share_send(j):
        for i, (d, jj) in enumerate(share_order):
            if jj == j:
                push(share0[i], chunk(0, z_of(1 - d, j)), x_dev)

    def share_wait():
        for i, (d, j) in enumerate(share_order):
            pushed(share0[i], chunk(0, z_of(1 - d, j), None, other))

    row = lax.broadcasted_iota(jnp.int32, (256, 256), 0)
    col = lax.broadcasted_iota(jnp.int32, (256, 256), 1)
    far_off = jnp.where(c < 2, 1e30, 0.0).astype(F32)
    near_off = jnp.where(c < 1, 1e30, 0.0).astype(F32)

    def attention(a, rb):
        ac = pl.ds(a * ADIM, ADIM)
        window = pl.ds(rb * 256, 1280)
        scores = nt(q[pl.ds(rb * 256, 256), ac], kv[0, window, ac])
        offs = (far_off, far_off, near_off, near_off, None, None)[rb:rb + 5]
        blocks = [scores[:, 256 * b:256 * b + 256] for b in range(5)]
        blocks[0] = jnp.where(col > row, blocks[0], -1e30)
        blocks[4] = jnp.where(col <= row, blocks[4], -1e30)
        top = None
        for block, off in zip(blocks, offs):
            peak = jnp.max(block, axis=1, keepdims=True)
            if off is not None:
                peak = peak - off
            top = peak if top is None else jnp.maximum(top, peak)
        base = top * SCALE
        weights = []
        for block, off in zip(blocks, offs):
            weights.append(jnp.exp2(block * SCALE - (base if off is None else base + off)))
        total = sum(jnp.sum(w, axis=1, keepdims=True) for w in weights)
        probs = jnp.concatenate([w.astype(BF) for w in weights], axis=1)
        mixed = nn(probs, kv[1, window, ac])
        att[pl.ds(rb * 256, 256), ac] = mixed / total

    def attend(strand):
        for a in (2 * strand, 2 * strand + 1):
            for rb in (0, 1):
                attention(a, rb)

    def apply(h):
        hc = pl.ds(h * HD, HD)
        queries = q[:, hc]
        gate = nt(queries, mi[h, 0:FH])
        up = nt(queries, mi[h, FH:2 * FH])
        hidden = (gate * jax.nn.sigmoid(gate) * up).astype(BF)
        old = wo[h].astype(F32)
        new = mo[h].astype(F32)
        old_norm = jnp.sqrt(jnp.sum(old * old, axis=0, keepdims=True))
        new_norm = jnp.sqrt(jnp.sum(new * new, axis=0, keepdims=True))
        applied = nn(hidden, mo[h]) * (old_norm / (new_norm + EPS))
        out[:, hc] = (att[:, hc] + applied).astype(BF)

    plus_start(0)
    minus_start(3)
    locals_[0].wait()
    locals_[1].wait()
    locals_[2].wait()
    gradients(0)
    cross0_start()
    plus_start(1)
    minus_start(4)
    gradients(1)
    ring1_step(0)
    plus_start(2)
    ring1_step(1)
    plus_cross_near(0)
    plus_forward(0)
    ring1_step(2)
    minus_second(3)
    ring1_step(3)
    ring0_step(0)
    ring1_end()
    plus_cross_near(1)
    plus_forward(1)
    minus_second(4)
    ring0_step(1)
    plus_cross_far(0)
    plus_cross_near(2)
    ring0_step(2)
    minus_third(3)
    plus_forward(2)
    ring0_step(3)
    ring0_end()
    y_reduce()
    renorm()
    y_gather()
    gather_send(0, 1)
    push(share1, chunk(1, z, None, x), x_dev)
    share_send(0)
    plus_cross_far(1)
    minus_third(4)
    pushed(share1, chunk(1, z, None, other))
    gather_send(1, 1)
    locals_[3].wait()
    plus_done(0)
    for j in (1, 2, 3):
        gather_wait(0, j)
        gather_send(0, j + 1)
        share_send(j)
        if j == 1:
            plus_cross_far(2)
            minus_cross(3)
        if j == 2:
            minus_cross(4)
        gather_wait(1, j)
        gather_send(1, j + 1)
    gather_wait(0, 4)
    share_send(4)
    attend(0)
    plus_done(1)
    attend(1)
    plus_done(2)
    attend(2)
    minus_done(3)
    attend(3)
    minus_done(4)
    attend(4)
    gather_wait(1, 4)
    apply(1)
    share_wait()
    apply(0)
    halo_sends_done()
    for index, ref in sent:
        copy(index, ref, ref, x_dev).wait_send()


def local(qkv, step_size, fast_in, fast_out):
    anywhere = pl.BlockSpec(memory_space=pl.ANY)
    vmem = pl.BlockSpec(memory_space=pltpu.VMEM)
    return pl.pallas_call(
        kernel,
        out_shape=jax.ShapeDtypeStruct((TOK, COLS), BF),
        in_specs=[anywhere, vmem, anywhere, anywhere],
        out_specs=vmem,
        scratch_shapes=[
            pltpu.VMEM((2, 3 * TOK, COLS), BF),
            pltpu.VMEM((TOK, COLS), BF),
            pltpu.VMEM((2, 2 * FH, HD), BF),
            pltpu.VMEM((2, FH, HD), BF),
            pltpu.VMEM((2, 16, 96, HD), BF),
            pltpu.VMEM((2, 2 * FH, HD), BF),
            pltpu.VMEM((2, FH, HD), BF),
            pltpu.VMEM((2, 2, 4, 96, HD), BF),
            pltpu.VMEM((2, 2, 4, 48, HD), BF),
            pltpu.VMEM((8, 96, HD), BF),
            pltpu.VMEM((96, HD), BF),
            pltpu.VMEM((96, HD), BF),
            pltpu.VMEM((96, HD), F32),
            pltpu.VMEM((96, HD), F32),
            pltpu.VMEM((4, 48, HD), BF),
            pltpu.VMEM((3, 48, HD), BF),
            pltpu.VMEM((3, 2, 2, TOK, STRAND), BF),
            pltpu.VMEM((2, 3, 2, TOK, STRAND), BF),
            pltpu.VMEM((TOK, COLS), F32),
            pltpu.SemaphoreType.DMA((4,)),
            pltpu.SemaphoreType.DMA((MESSAGES,)),
            pltpu.SemaphoreType.DMA((MESSAGES,)),
        ],
        name="ttt_layer",
        compiler_params=pltpu.CompilerParams(
            collective_id=0, has_side_effects=True, vmem_limit_bytes=62 * 2**20
        ),
    )(qkv, step_size, fast_in.transpose(0, 2, 1), fast_out)


def solution(mesh):
    placed = (
        P(None, "ctx", "head"),
        P("ctx", "head"),
        P("head", None, None),
        P("head", None, None),
    )
    return jax.shard_map(
        local, mesh=mesh, in_specs=placed, out_specs=P("ctx", "head"), check_vma=False
    )
```

```python
import functools

import jax
import jax.numpy as jnp
from jax import lax
from jax.experimental import pallas as pl
from jax.experimental.pallas import tpu as pltpu
from jax.sharding import PartitionSpec as P

ADIM = 128
FH = 512
HD = 640
TOK = 512
COLS = 1280
EPS = 1e-06
FACTOR = 32768.0 ** -0.5
SCALE = 1.4426950408889634 * ADIM ** -0.5
STRAND = 256
PLUS = (0, 1, 2)
MINUS = (3, 4)
CROSS_NEAR_FIRST = {0: True, 1: False, 2: True}
CROSS_FAR_FIRST = {0: False, 1: True, 2: True}
BF = jnp.bfloat16
F32 = jnp.float32
MESH = pl.DeviceIdType.MESH
MESSAGES = 160


def nt(a, b):
    return lax.dot_general(a, b, (((1,), (1,)), ((), ())), preferred_element_type=F32)


def nn(a, b):
    return jnp.dot(a, b, preferred_element_type=F32)


def mult(index, of):
    return pl.multiple_of(index, of)


def kernel(
    qkv, step, w_in, w_out, out,
    kv, q, wi, wo, g, mi, mo, r1, r0, xb, x1, t1, u0, u1, ys, yr, pst, sst, att,
    local_sem, ss, rs,
):
    c = lax.axis_index("ctx")
    head = lax.axis_index("head")
    y = lax.rem(c, 4)
    x = lax.rem(c // 4, 2)
    z = c // 8
    other = 1 - x
    s_own = 2 * z + x

    def at(zz, xx, yy):
        return (8 * lax.rem(zz + 16, 8) + 4 * xx + lax.rem(yy + 8, 4), head)

    y_dev = {j: at(z, x, y + j) for j in (-1, 1, 2, 3)}
    z_dev = (at(z + 1, x, y), at(z - 1, x, y))
    x_dev = at(z, other, y)
    next_dev = (lax.rem(c + 4, 64), head)
    prev_dev = (lax.rem(c + 60, 64), head)

    used = [0]
    sent = []

    def message(size_ref, always=True):
        index = used[0]
        used[0] += 1
        if always:
            sent.append((index, size_ref))
        return index

    def copy(index, src, dst, device):
        return pltpu.make_async_remote_copy(
            src_ref=src, dst_ref=dst, send_sem=ss.at[index], recv_sem=rs.at[index],
            device_id=device, device_id_type=MESH,
        )

    def landed(index, ref):
        copy(index, ref, ref, x_dev).wait_recv()

    barrier = pltpu.get_barrier_semaphore()
    for device in (y_dev[1], y_dev[2], y_dev[3], *z_dev, x_dev, next_dev, prev_dev):
        pl.semaphore_signal(barrier, inc=1, device_id=device, device_id_type=MESH)

    locals_ = []

    def fetch(src, dst):
        cp = pltpu.make_async_copy(src, dst, local_sem.at[len(locals_)])
        cp.start()
        locals_.append(cp)

    own_rows = pl.ds(2 * TOK, TOK)
    near_rows = pl.ds(TOK, TOK)
    far_rows = pl.ds(0, TOK)
    fetch(qkv.at[pl.ds(1, 2)], kv.at[:, own_rows])
    fetch(w_in, wi)
    fetch(w_out, wo)
    fetch(qkv.at[0], q)
    pl.semaphore_wait(barrier, 8)

    def cols(strand):
        return pl.ds(strand * STRAND, STRAND)

    def own(strand):
        return qkv.at[pl.ds(1, 2), :, cols(strand)]

    def near(strand):
        return kv.at[:, near_rows, cols(strand)]

    def far(strand):
        return kv.at[:, far_rows, cols(strand)]

    pid = {}
    for strand in PLUS:
        for name in ("near", "far", "c3", "c2", "xnear", "xfar"):
            pid[strand, name] = message(None, False)
    for strand in MINUS:
        for name in ("u1", "u2", "u3", "cfar"):
            pid[strand, name] = message(None, False)

    def halo(strand, name, src, dst, device):
        copy(pid[strand, name], src, dst, device).start()

    def plus_start(strand, last=True, rest=True):
        if rest:
            @pl.when(y < 3)
            def _():
                halo(strand, "near", own(strand), near(strand), y_dev[1])

        if last:
            @pl.when(y == 3)
            def _():
                halo(strand, "c3", own(strand), pst.at[strand, 0],
                     next_dev if CROSS_NEAR_FIRST[strand] else y_dev[1])

    def plus_relay_near(strand):
        if CROSS_NEAR_FIRST[strand]:
            @pl.when(y == 3)
            def _():
                landed(pid[strand, "c3"], pst.at[strand, 0])
                halo(strand, "near", pst.at[strand, 0], near(strand), y_dev[1])
        else:
            @pl.when(y == 0)
            def _():
                landed(pid[strand, "c3"], pst.at[strand, 0])
                halo(strand, "xnear", pst.at[strand, 0], near(strand), next_dev)

    def plus_relay_far(strand):
        if CROSS_FAR_FIRST[strand]:
            @pl.when(y == 3)
            def _():
                landed(pid[strand, "c2"], pst.at[strand, 1])
                halo(strand, "far", pst.at[strand, 1], far(strand), y_dev[1])
        else:
            @pl.when(y == 0)
            def _():
                landed(pid[strand, "c2"], pst.at[strand, 1])
                halo(strand, "xfar", pst.at[strand, 1], far(strand), next_dev)

    def plus_forward(strand, ys_=(0, 1, 2, 3)):
        for yy in ys_:
            @pl.when(y == yy)
            def _():
                late = yy == 0 and not CROSS_NEAR_FIRST[strand]
                landed(pid[strand, "xnear" if late else "near"], near(strand))
                if yy < 3:
                    halo(strand, "far", near(strand), far(strand), y_dev[1])
                else:
                    halo(strand, "c2", near(strand), pst.at[strand, 1],
                         next_dev if CROSS_FAR_FIRST[strand] else y_dev[1])

    def plus_done(strand):
        if CROSS_FAR_FIRST[strand]:
            landed(pid[strand, "far"], far(strand))
        else:
            @pl.when(y == 0)
            def _():
                landed(pid[strand, "xfar"], far(strand))

            @pl.when(y > 0)
            def _():
                landed(pid[strand, "far"], far(strand))

    def minus_start(strand):
        halo(strand, "u1", own(strand), sst.at[strand - MINUS[0], 0], y_dev[-1])

    def minus_second(strand):
        m = strand - MINUS[0]
        landed(pid[strand, "u1"], sst.at[m, 0])

        @pl.when((y == 0) | (y == 3))
        def _():
            halo(strand, "u2", sst.at[m, 0], far(strand), y_dev[-1])

        @pl.when((y == 1) | (y == 2))
        def _():
            halo(strand, "u2", sst.at[m, 0], sst.at[m, 1], y_dev[-1])

    def minus_hand(strand):
        m = strand - MINUS[0]

        @pl.when(y <= 1)
        def _():
            landed(pid[strand, "u2"], sst.at[m, 1])
            halo(strand, "cfar", sst.at[m, 1], far(strand), next_dev)

    def minus_third(strand):
        m = strand - MINUS[0]

        @pl.when(y >= 2)
        def _():
            landed(pid[strand, "u2"], far(strand))
            halo(strand, "u3", far(strand), near(strand), y_dev[-1])

        @pl.when(y == 0)
        def _():
            halo(strand, "u3", sst.at[m, 1], near(strand), y_dev[-1])

    def minus_cross(strand):
        @pl.when(y == 1)
        def _():
            landed(pid[strand, "cfar"], far(strand))
            halo(strand, "u3", far(strand), near(strand), y_dev[-1])

    def minus_done(strand):
        landed(pid[strand, "u3"], near(strand))

        @pl.when(y == 0)
        def _():
            landed(pid[strand, "cfar"], far(strand))

    def halo_sends_done():
        def done(condition, *which):
            def wait():
                for strand, name in which:
                    copy(pid[strand, name], near(strand), near(strand), x_dev).wait_send()

            if condition is None:
                wait()
            else:
                pl.when(condition)(wait)

        for strand in PLUS:
            done(y == 3, (strand, "c3"), (strand, "c2"))
            if CROSS_NEAR_FIRST[strand]:
                done(None, (strand, "near"))
            else:
                done(y < 3, (strand, "near"))
                done(y == 0, (strand, "xnear"))
            if CROSS_FAR_FIRST[strand]:
                done(None, (strand, "far"))
            else:
                done(y < 3, (strand, "far"))
                done(y == 0, (strand, "xfar"))
        for strand in MINUS:
            done(None, (strand, "u1"), (strand, "u2"), (strand, "u3"))
            done(y <= 1, (strand, "cfar"))

    def gradients(h):
        hc = pl.ds(h * HD, HD)
        keys = kv[0, own_rows, hc]
        vals = kv[1, own_rows, hc]
        rate = step[:, h:h + 1]
        scaled = (rate * vals.astype(F32)).astype(BF)
        gate = nt(wi[h, 0:FH], keys)
        up = nt(wi[h, FH:2 * FH], keys)
        back = nt(wo[h], scaled)
        sig = jax.nn.sigmoid(gate)
        act = gate * sig
        hidden = (act * up).astype(BF)
        d_gate = (back * up * sig * (1.0 + gate * (1.0 - sig))).astype(BF)
        d_up = (back * act).astype(BF)
        g_gate = nn(d_gate, keys).astype(BF)
        for s in range(8):
            g[h, s, 0:64] = g_gate[64 * s:64 * s + 64]
        g_up = nn(d_up, keys).astype(BF)
        for s in range(8):
            g[h, 8 + s, 0:64] = g_up[64 * s:64 * s + 64]
        g_out = nn(hidden, scaled).astype(BF)
        for s in range(16):
            g[h, s, 64:96] = g_out[32 * s:32 * s + 32]

    def add(dst, src):
        dst[...] = (dst[...].astype(F32) + src[...].astype(F32)).astype(BF)

    def z_of(direction, distance):
        offset = distance if direction == 0 else -distance
        return lax.rem(z + offset + 8, 8)

    def chains(k):
        for direction in (0, 1):
            for half in (direction, 1 - direction):
                start = 0 if half == direction else 1
                if k >= start:
                    yield direction, half, k == start

    ring1 = {(d, h, k): message(r1.at[0, 0, 0]) for k in range(4) for d, h, _ in chains(k)}
    ring0 = {(d, h, k): message(r0.at[0, 0, 0]) for k in range(4) for d, h, _ in chains(k)}
    cross0 = [message(xb.at[0]) for _ in range(8)]
    cross1 = message(x1)

    def ring1_step(k):
        for direction, half, first in chains(k):
            part = g.at[1, 2 * z_of(direction, 4 - k) + half]
            if first:
                src = part
            else:
                src = r1.at[direction, half, k - 1]
                landed(ring1[direction, half, k - 1], src)
                add(src, part)
            copy(ring1[direction, half, k], src, r1.at[direction, half, k], z_dev[direction]).start()

    def ring1_end():
        for direction in (0, 1):
            for half in (0, 1):
                landed(ring1[direction, half, 3], r1.at[direction, half, 3])

        def total(half):
            return (
                g[1, 2 * z + half].astype(F32)
                + r1[0, half, 3].astype(F32)
                + r1[1, half, 3].astype(F32)
            )

        t1[...] = total(other).astype(BF)
        copy(cross1, t1, x1, x_dev).start()
        u1[...] = total(x)

    slots = [(0, 4), (0, 3), (1, 3), (0, 2), (1, 2), (0, 1), (1, 1), (0, 0)]
    slot_of = {pair: i for i, pair in enumerate(slots)}
    slot_of[1, 4] = 0

    def cross0_start():
        for i, (direction, distance) in enumerate(slots):
            copy(
                cross0[i], g.at[0, 2 * z_of(direction, distance) + other], xb.at[i], x_dev
            ).start()

    def cross0_add(i):
        landed(cross0[i], xb.at[i])
        direction, distance = slots[i]
        add(xb.at[i], g.at[0, 2 * z_of(direction, distance) + x])

    def ring0_step(k):
        for i in {0: (0,), 1: (1, 2), 2: (3, 4), 3: (5, 6)}[k]:
            cross0_add(i)
        for direction, half, first in chains(k):
            part = xb.at[slot_of[direction, 4 - k], pl.ds(48 * half, 48)]
            if first:
                src = part
            else:
                src = r0.at[direction, half, k - 1]
                landed(ring0[direction, half, k - 1], src)
                add(src, part)
            copy(ring0[direction, half, k], src, r0.at[direction, half, k], z_dev[direction]).start()

    def ring0_end():
        cross0_add(7)
        for half in (0, 1):
            rows = pl.ds(48 * half, 48)
            for direction in (0, 1):
                landed(ring0[direction, half, 3], r0.at[direction, half, 3])
            u0[rows] = (
                xb[7, rows].astype(F32) + r0[0, half, 3].astype(F32) + r0[1, half, 3].astype(F32)
            )

    y_sum = {j: message(ys.at[0]) for j in (1, 2, 3)}

    def y_reduce():
        landed(cross1, x1)
        u1[...] = u1[...] + x1[...].astype(F32)
        for p in range(4):
            ys[p, 0:16] = u0[16 * p:16 * p + 16].astype(BF)
            ys[p, 16:32] = u1[16 * p:16 * p + 16].astype(BF)
            source = u0 if p < 2 else u1
            first = 64 + 16 * (p % 2)
            ys[p, 32:48] = source[first:first + 16].astype(BF)
        for j in (1, 2, 3):
            copy(y_sum[j], ys.at[lax.rem(y + j, 4)], yr.at[j - 1], y_dev[j]).start()
        for j in (1, 2, 3):
            landed(y_sum[j], yr.at[j - 1])

    in_row = mult(64 * s_own + 16 * y, 16)
    out_head = y // 2
    out_row = mult(32 * s_own + 16 * lax.rem(y, 2), 16)

    def renorm():
        in_piece = pl.ds(mult(16 * y, 16), 16)
        out_piece = pl.ds(mult(64 + 16 * lax.rem(y, 2), 16), 16)
        total = jnp.concatenate(
            [u0[in_piece], u1[in_piece], jnp.where(y < 2, u0[out_piece], u1[out_piece])], axis=0
        )
        for j in range(3):
            total = total + yr[j].astype(F32)
        for h in (0, 1):
            old = wi[h, pl.ds(in_row, 16)].astype(F32)
            moved = old + total[16 * h:16 * h + 16] * FACTOR
            old_norm = jnp.sqrt(jnp.sum(old * old, axis=1, keepdims=True))
            new_norm = jnp.sqrt(jnp.sum(moved * moved, axis=1, keepdims=True))
            mi[h, pl.ds(in_row, 16)] = (moved * (old_norm / (new_norm + EPS))).astype(BF)
        old = wo[out_head, pl.ds(out_row, 16)].astype(F32)
        mo[out_head, pl.ds(out_row, 16)] = (old + total[32:48] * FACTOR).astype(BF)

    sixteen = mi.at[0, pl.ds(0, 16)]
    y_all = {(j, i): message(sixteen) for j in (1, 2, 3) for i in range(3)}

    def y_gather():
        pieces = (
            mi.at[0, pl.ds(in_row, 16)],
            mi.at[1, pl.ds(in_row, 16)],
            mo.at[out_head, pl.ds(out_row, 16)],
        )
        for j in (1, 2, 3):
            for i, piece in enumerate(pieces):
                copy(y_all[j, i], piece, piece, y_dev[j]).start()
        for j in (1, 2, 3):
            yy = lax.rem(y - j + 4, 4)
            row = mult(64 * s_own + 16 * yy, 16)
            landed(y_all[j, 0], mi.at[0, pl.ds(row, 16)])
            landed(y_all[j, 1], mi.at[1, pl.ds(row, 16)])
            row = mult(32 * s_own + 16 * lax.rem(yy, 2), 16)
            landed(y_all[j, 2], mo.at[yy // 2, pl.ds(row, 16)])

    def chunk(h, zz, part=None, xx=None):
        rows = 128 if h == 1 else 64
        first = 128 * zz + (64 * (x if xx is None else xx) if h == 0 or xx is not None else 0)
        if xx is not None:
            rows = 64
        n_in, f_in = rows, first
        n_out, f_out = rows // 2, first // 2
        if part is not None:
            n_in, n_out = n_in // 2, n_out // 2
            f_in = f_in + part * n_in
            f_out = f_out + part * n_out
        return (
            mi.at[h, pl.ds(mult(f_in, 16), n_in)],
            mo.at[h, pl.ds(mult(f_out, 16), n_out)],
        )

    def pair_ids(h, part=None, xx=None):
        return tuple(message(ref) for ref in chunk(h, 0, part, xx))

    def push(ids, refs, device):
        for index, ref in zip(ids, refs):
            copy(index, ref, ref, device).start()

    def pushed(ids, refs):
        for index, ref in zip(ids, refs):
            landed(index, ref)

    gather = {
        (h, j, d): pair_ids(h, d if j == 4 else None)
        for h in (0, 1) for j in (1, 2, 3, 4) for d in (0, 1)
    }
    share0 = [pair_ids(0) for _ in range(8)]
    share1 = pair_ids(1, None, x)

    def gather_send(h, j):
        for d in (0, 1):
            part = d if j == 4 else None
            push(gather[h, j, d], chunk(h, z_of(1 - d, j - 1), part), z_dev[d])

    def gather_wait(h, j):
        for d in (0, 1):
            part = d if j == 4 else None
            pushed(gather[h, j, d], chunk(h, z_of(1 - d, j), part))

    share_order = [(0, 0)] + [(d, j) for j in (1, 2, 3) for d in (0, 1)] + [(0, 4)]

    def share_send(j):
        for i, (d, jj) in enumerate(share_order):
            if jj == j:
                push(share0[i], chunk(0, z_of(1 - d, j)), x_dev)

    def share_wait():
        for i, (d, j) in enumerate(share_order):
            pushed(share0[i], chunk(0, z_of(1 - d, j), None, other))

    row = lax.broadcasted_iota(jnp.int32, (256, 256), 0)
    col = lax.broadcasted_iota(jnp.int32, (256, 256), 1)
    far_off = jnp.where(c < 2, 1e30, 0.0).astype(F32)
    near_off = jnp.where(c < 1, 1e30, 0.0).astype(F32)

    attended_heads = set()
    applied_heads = set()

    def attention(a, rb):
        ac = pl.ds(a * ADIM, ADIM)
        window = pl.ds(rb * 256, 1280)
        scores = nt(q[pl.ds(rb * 256, 256), ac], kv[0, window, ac])
        offs = (far_off, far_off, near_off, near_off, None, None)[rb:rb + 5]
        blocks = [scores[:, 256 * b:256 * b + 256] for b in range(5)]
        blocks[0] = jnp.where(col > row, blocks[0], -1e30)
        blocks[4] = jnp.where(col <= row, blocks[4], -1e30)
        top = None
        for block, off in zip(blocks, offs):
            peak = jnp.max(block, axis=1, keepdims=True)
            if off is not None:
                peak = peak - off
            top = peak if top is None else jnp.maximum(top, peak)
        base = top * SCALE
        weights = []
        for block, off in zip(blocks, offs):
            weights.append(jnp.exp2(block * SCALE - (base if off is None else base + off)))
        total = sum(jnp.sum(w, axis=1, keepdims=True) for w in weights)
        probs = jnp.concatenate([w.astype(BF) for w in weights], axis=1)
        mixed = nn(probs, kv[1, window, ac])
        rows = pl.ds(rb * 256, 256)
        if a // 5 in applied_heads:
            out[rows, ac] = (att[rows, ac] + mixed / total).astype(BF)
        else:
            att[rows, ac] = mixed / total
        attended_heads.add(a)

    def attend(strand):
        for a in (2 * strand, 2 * strand + 1):
            for rb in (0, 1):
                attention(a, rb)

    def apply(h):
        hc = pl.ds(h * HD, HD)
        queries = q[:, hc]
        gate = nt(queries, mi[h, 0:FH])
        up = nt(queries, mi[h, FH:2 * FH])
        hidden = (gate * jax.nn.sigmoid(gate) * up).astype(BF)
        old = wo[h].astype(F32)
        new = mo[h].astype(F32)
        old_norm = jnp.sqrt(jnp.sum(old * old, axis=0, keepdims=True))
        new_norm = jnp.sqrt(jnp.sum(new * new, axis=0, keepdims=True))
        applied = nn(hidden, mo[h]) * (old_norm / (new_norm + EPS))
        for a in range(5 * h, 5 * h + 5):
            ac = pl.ds(a * ADIM, ADIM)
            part = applied[:, (a - 5 * h) * ADIM:(a - 5 * h + 1) * ADIM]
            if a in attended_heads:
                out[:, ac] = (att[:, ac] + part).astype(BF)
            else:
                att[:, ac] = part
        applied_heads.add(h)

    plus_start(0)
    minus_start(3)
    plus_start(1, rest=False)
    locals_[0].wait()
    locals_[1].wait()
    locals_[2].wait()
    gradients(0)
    cross0_start()
    plus_start(1, last=False)
    minus_start(4)
    gradients(1)
    ring1_step(0)
    ring1_step(1)
    plus_relay_near(0)
    plus_relay_near(1)
    plus_forward(0, (1, 2, 3))
    minus_second(3)
    ring1_step(2)
    ring1_step(3)
    plus_forward(0, (0,))
    ring0_step(0)
    ring0_step(1)
    ring1_end()
    plus_start(2, rest=False)
    plus_forward(1, (3,))
    ring0_step(2)
    minus_hand(3)
    plus_relay_far(0)
    ring0_step(3)
    ring0_end()
    y_reduce()
    renorm()
    y_gather()
    gather_send(0, 1)
    push(share1, chunk(1, z, None, x), x_dev)
    share_send(0)
    plus_start(2, last=False)
    plus_relay_near(2)
    minus_third(3)
    minus_second(4)
    plus_forward(1, (0, 1, 2))
    minus_cross(3)
    pushed(share1, chunk(1, z, None, other))
    gather_send(1, 1)
    locals_[3].wait()
    for j in (1, 2, 3):
        gather_wait(0, j)
        gather_send(0, j + 1)
        share_send(j)
        gather_wait(1, j)
        gather_send(1, j + 1)
        if j == 1:
            plus_relay_far(1)
        if j == 2:
            plus_done(0)
            attend(0)
            minus_hand(4)
            minus_third(4)
            plus_forward(2)
        if j == 3:
            minus_done(3)
            attend(3)
    gather_wait(0, 4)
    share_send(4)
    plus_done(1)
    attend(1)
    plus_relay_far(2)
    minus_cross(4)
    gather_wait(1, 4)
    apply(1)
    minus_done(4)
    attend(4)
    plus_done(2)
    attend(2)
    share_wait()
    apply(0)
    halo_sends_done()
    for index, ref in sent:
        copy(index, ref, ref, x_dev).wait_send()


def local(qkv, step_size, fast_in, fast_out):
    anywhere = pl.BlockSpec(memory_space=pl.ANY)
    vmem = pl.BlockSpec(memory_space=pltpu.VMEM)
    return pl.pallas_call(
        kernel,
        out_shape=jax.ShapeDtypeStruct((TOK, COLS), BF),
        in_specs=[anywhere, vmem, anywhere, anywhere],
        out_specs=vmem,
        scratch_shapes=[
            pltpu.VMEM((2, 3 * TOK, COLS), BF),
            pltpu.VMEM((TOK, COLS), BF),
            pltpu.VMEM((2, 2 * FH, HD), BF),
            pltpu.VMEM((2, FH, HD), BF),
            pltpu.VMEM((2, 16, 96, HD), BF),
            pltpu.VMEM((2, 2 * FH, HD), BF),
            pltpu.VMEM((2, FH, HD), BF),
            pltpu.VMEM((2, 2, 4, 96, HD), BF),
            pltpu.VMEM((2, 2, 4, 48, HD), BF),
            pltpu.VMEM((8, 96, HD), BF),
            pltpu.VMEM((96, HD), BF),
            pltpu.VMEM((96, HD), BF),
            pltpu.VMEM((96, HD), F32),
            pltpu.VMEM((96, HD), F32),
            pltpu.VMEM((4, 48, HD), BF),
            pltpu.VMEM((3, 48, HD), BF),
            pltpu.VMEM((3, 2, 2, TOK, STRAND), BF),
            pltpu.VMEM((2, 2, 2, TOK, STRAND), BF),
            pltpu.VMEM((TOK, COLS), F32),
            pltpu.SemaphoreType.DMA((4,)),
            pltpu.SemaphoreType.DMA((MESSAGES,)),
            pltpu.SemaphoreType.DMA((MESSAGES,)),
        ],
        name="ttt_layer",
        compiler_params=pltpu.CompilerParams(
            collective_id=0, has_side_effects=True, vmem_limit_bytes=62 * 2**20
        ),
    )(qkv, step_size, fast_in.transpose(0, 2, 1), fast_out)


def solution(mesh):
    placed = (
        P(None, "ctx", "head"),
        P("ctx", "head"),
        P("head", None, None),
        P("head", None, None),
    )
    return jax.shard_map(
        local, mesh=mesh, in_specs=placed, out_specs=P("ctx", "head"), check_vma=False
    )
```

```python
import functools

import jax
import jax.numpy as jnp
from jax import lax
from jax.experimental import pallas as pl
from jax.experimental.pallas import tpu as pltpu
from jax.sharding import PartitionSpec as P

ADIM = 128
FH = 512
HD = 640
TOK = 512
COLS = 1280
EPS = 1e-06
FACTOR = 32768.0 ** -0.5
SCALE = 1.4426950408889634 * ADIM ** -0.5
STRAND = 256
PLUS = (0, 1, 2)
MINUS = (3, 4)
CROSS_NEAR_FIRST = {0: True, 1: False, 2: True}
CROSS_FAR_FIRST = {0: False, 1: True, 2: True}
VIA = {(1, "c2"): 0, (0, "xfar"): 1, (3, "cfar"): 2}
BF = jnp.bfloat16
F32 = jnp.float32
MESH = pl.DeviceIdType.MESH
MESSAGES = 160


def nt(a, b):
    return lax.dot_general(a, b, (((1,), (1,)), ((), ())), preferred_element_type=F32)


def nn(a, b):
    return jnp.dot(a, b, preferred_element_type=F32)


def mult(index, of):
    return pl.multiple_of(index, of)


def kernel(
    qkv, step, w_in, w_out, out,
    kv, q, wi, wo, g, mi, mo, r1, r0, xb, x1, t1, u0, u1, ys, yr, pst, sst, vst, att,
    local_sem, ss, rs,
):
    c = lax.axis_index("ctx")
    head = lax.axis_index("head")
    y = lax.rem(c, 4)
    x = lax.rem(c // 4, 2)
    z = c // 8
    other = 1 - x
    s_own = 2 * z + x

    def at(zz, xx, yy):
        return (8 * lax.rem(zz + 16, 8) + 4 * xx + lax.rem(yy + 8, 4), head)

    y_dev = {j: at(z, x, y + j) for j in (-1, 1, 2, 3)}
    z_dev = (at(z + 1, x, y), at(z - 1, x, y))
    x_dev = at(z, other, y)
    next_dev = (lax.rem(c + 4, 64), head)
    prev_dev = (lax.rem(c + 60, 64), head)

    used = [0]
    sent = []

    def message(size_ref, always=True):
        index = used[0]
        used[0] += 1
        if always:
            sent.append((index, size_ref))
        return index

    def copy(index, src, dst, device):
        return pltpu.make_async_remote_copy(
            src_ref=src, dst_ref=dst, send_sem=ss.at[index], recv_sem=rs.at[index],
            device_id=device, device_id_type=MESH,
        )

    def landed(index, ref):
        copy(index, ref, ref, x_dev).wait_recv()

    barrier = pltpu.get_barrier_semaphore()
    for device in (y_dev[1], y_dev[2], y_dev[3], *z_dev, x_dev, next_dev, prev_dev):
        pl.semaphore_signal(barrier, inc=1, device_id=device, device_id_type=MESH)

    locals_ = []

    def fetch(src, dst):
        cp = pltpu.make_async_copy(src, dst, local_sem.at[len(locals_)])
        cp.start()
        locals_.append(cp)

    own_rows = pl.ds(2 * TOK, TOK)
    near_rows = pl.ds(TOK, TOK)
    far_rows = pl.ds(0, TOK)
    fetch(qkv.at[pl.ds(1, 2)], kv.at[:, own_rows])
    fetch(w_in, wi)
    fetch(w_out, wo)
    fetch(qkv.at[0], q)
    pl.semaphore_wait(barrier, 8)

    def cols(strand):
        return pl.ds(strand * STRAND, STRAND)

    def own(strand):
        return qkv.at[pl.ds(1, 2), :, cols(strand)]

    def near(strand):
        return kv.at[:, near_rows, cols(strand)]

    def far(strand):
        return kv.at[:, far_rows, cols(strand)]

    pid = {}
    for strand in PLUS:
        for name in ("near", "far", "c3", "c2", "xnear", "xfar"):
            pid[strand, name] = message(None, False)
    for strand in MINUS:
        for name in ("u1", "u2", "u3", "cfar"):
            pid[strand, name] = message(None, False)

    for strand, name in VIA:
        for leg in ("v", "r"):
            pid[strand, name + leg] = message(None, False)

    def halo(strand, name, src, dst, device):
        copy(pid[strand, name], src, dst, device).start()

    def cross(strand, name, src, dst):
        if (strand, name) not in VIA:
            halo(strand, name, src, dst, next_dev)
            return

        @pl.when(x == 0)
        def _():
            halo(strand, name, src, dst, next_dev)

        @pl.when(x == 1)
        def _():
            halo(strand, name + "v", src, vst.at[VIA[strand, name]], x_dev)

    def relay(strand, name, where, dst):
        if (strand, name) not in VIA:
            return

        @pl.when((x == 0) & where)
        def _():
            stage = vst.at[VIA[strand, name]]
            landed(pid[strand, name + "v"], stage)
            halo(strand, name + "r", stage, dst, z_dev[0])

    def crossed(strand, name, dst):
        if (strand, name) not in VIA:
            landed(pid[strand, name], dst)
            return

        @pl.when(x == 0)
        def _():
            landed(pid[strand, name + "r"], dst)

        @pl.when(x == 1)
        def _():
            landed(pid[strand, name], dst)

    def plus_start(strand, last=True, rest=True):
        if rest:
            @pl.when(y < 3)
            def _():
                halo(strand, "near", own(strand), near(strand), y_dev[1])

        if last:
            @pl.when(y == 3)
            def _():
                halo(strand, "c3", own(strand), pst.at[strand, 0],
                     next_dev if CROSS_NEAR_FIRST[strand] else y_dev[1])

    def plus_relay_near(strand):
        if CROSS_NEAR_FIRST[strand]:
            @pl.when(y == 3)
            def _():
                landed(pid[strand, "c3"], pst.at[strand, 0])
                halo(strand, "near", pst.at[strand, 0], near(strand), y_dev[1])
        else:
            @pl.when(y == 0)
            def _():
                landed(pid[strand, "c3"], pst.at[strand, 0])
                halo(strand, "xnear", pst.at[strand, 0], near(strand), next_dev)

    def plus_relay_far(strand):
        if CROSS_FAR_FIRST[strand]:
            @pl.when(y == 3)
            def _():
                crossed(strand, "c2", pst.at[strand, 1])
                halo(strand, "far", pst.at[strand, 1], far(strand), y_dev[1])
        else:
            @pl.when(y == 0)
            def _():
                landed(pid[strand, "c2"], pst.at[strand, 1])
                cross(strand, "xfar", pst.at[strand, 1], far(strand))

    def plus_forward(strand, ys_=(0, 1, 2, 3)):
        for yy in ys_:
            @pl.when(y == yy)
            def _():
                late = yy == 0 and not CROSS_NEAR_FIRST[strand]
                landed(pid[strand, "xnear" if late else "near"], near(strand))
                if yy < 3:
                    halo(strand, "far", near(strand), far(strand), y_dev[1])
                else:
                    if CROSS_FAR_FIRST[strand]:
                        cross(strand, "c2", near(strand), pst.at[strand, 1])
                    else:
                        halo(strand, "c2", near(strand), pst.at[strand, 1], y_dev[1])

    def plus_done(strand):
        if CROSS_FAR_FIRST[strand]:
            landed(pid[strand, "far"], far(strand))
        else:
            @pl.when(y == 0)
            def _():
                crossed(strand, "xfar", far(strand))

            @pl.when(y > 0)
            def _():
                landed(pid[strand, "far"], far(strand))

    def minus_start(strand):
        halo(strand, "u1", own(strand), sst.at[strand - MINUS[0], 0], y_dev[-1])

    def minus_second(strand):
        m = strand - MINUS[0]
        landed(pid[strand, "u1"], sst.at[m, 0])

        @pl.when((y == 0) | (y == 3))
        def _():
            halo(strand, "u2", sst.at[m, 0], far(strand), y_dev[-1])

        @pl.when((y == 1) | (y == 2))
        def _():
            halo(strand, "u2", sst.at[m, 0], sst.at[m, 1], y_dev[-1])

    def minus_hand(strand):
        m = strand - MINUS[0]

        @pl.when(y <= 1)
        def _():
            landed(pid[strand, "u2"], sst.at[m, 1])
            cross(strand, "cfar", sst.at[m, 1], far(strand))

    def minus_third(strand):
        m = strand - MINUS[0]

        @pl.when(y >= 2)
        def _():
            landed(pid[strand, "u2"], far(strand))
            halo(strand, "u3", far(strand), near(strand), y_dev[-1])

        @pl.when(y == 0)
        def _():
            halo(strand, "u3", sst.at[m, 1], near(strand), y_dev[-1])

    def minus_cross(strand):
        @pl.when(y == 1)
        def _():
            crossed(strand, "cfar", far(strand))
            halo(strand, "u3", far(strand), near(strand), y_dev[-1])

    def minus_done(strand):
        landed(pid[strand, "u3"], near(strand))

        @pl.when(y == 0)
        def _():
            crossed(strand, "cfar", far(strand))

    def halo_sends_done():
        def wait(condition, strand, name):
            @pl.when(condition)
            def _():
                copy(pid[strand, name], near(strand), near(strand), x_dev).wait_send()

        def done(condition, *which):
            for strand, name in which:
                if (strand, name) in VIA:
                    wait(condition & (x == 0), strand, name)
                    wait(condition & (x == 1), strand, name + "v")
                    wait(condition & (x == 0), strand, name + "r")
                else:
                    wait(y >= 0 if condition is None else condition, strand, name)

        for strand in PLUS:
            done(y == 3, (strand, "c3"), (strand, "c2"))
            if CROSS_NEAR_FIRST[strand]:
                done(None, (strand, "near"))
            else:
                done(y < 3, (strand, "near"))
                done(y == 0, (strand, "xnear"))
            if CROSS_FAR_FIRST[strand]:
                done(None, (strand, "far"))
            else:
                done(y < 3, (strand, "far"))
                done(y == 0, (strand, "xfar"))
        for strand in MINUS:
            done(None, (strand, "u1"), (strand, "u2"), (strand, "u3"))
            done(y <= 1, (strand, "cfar"))

    def gradients(h):
        hc = pl.ds(h * HD, HD)
        keys = kv[0, own_rows, hc]
        vals = kv[1, own_rows, hc]
        rate = jnp.broadcast_to(step[h:h + 1, :], (8, TOK)).T[:, 0:1]
        scaled = (rate * vals.astype(F32)).astype(BF)
        gate = nt(wi[h, 0:FH], keys)
        up = nt(wi[h, FH:2 * FH], keys)
        back = nt(wo[h], scaled)
        sig = jax.nn.sigmoid(gate)
        act = gate * sig
        hidden = (act * up).astype(BF)
        d_gate = (back * up * sig * (1.0 + gate * (1.0 - sig))).astype(BF)
        d_up = (back * act).astype(BF)
        g_gate = nn(d_gate, keys).astype(BF)
        for s in range(8):
            g[h, s, 0:64] = g_gate[64 * s:64 * s + 64]
        g_up = nn(d_up, keys).astype(BF)
        for s in range(8):
            g[h, 8 + s, 0:64] = g_up[64 * s:64 * s + 64]
        g_out = nn(hidden, scaled).astype(BF)
        for s in range(16):
            g[h, s, 64:96] = g_out[32 * s:32 * s + 32]

    def add(dst, src):
        dst[...] = (dst[...].astype(F32) + src[...].astype(F32)).astype(BF)

    def z_of(direction, distance):
        offset = distance if direction == 0 else -distance
        return lax.rem(z + offset + 8, 8)

    def chains(k):
        for direction in (0, 1):
            for half in (direction, 1 - direction):
                start = 0 if half == direction else 1
                if k >= start:
                    yield direction, half, k == start

    ring1 = {(d, h, k): message(r1.at[0, 0, 0]) for k in range(4) for d, h, _ in chains(k)}
    ring0 = {(d, h, k): message(r0.at[0, 0, 0]) for k in range(4) for d, h, _ in chains(k)}
    cross0 = [message(xb.at[0]) for _ in range(8)]
    cross1 = message(x1)

    def ring1_step(k):
        for direction, half, first in chains(k):
            part = g.at[1, 2 * z_of(direction, 4 - k) + half]
            if first:
                src = part
            else:
                src = r1.at[direction, half, k - 1]
                landed(ring1[direction, half, k - 1], src)
                add(src, part)
            copy(ring1[direction, half, k], src, r1.at[direction, half, k], z_dev[direction]).start()

    def ring1_end():
        for direction in (0, 1):
            for half in (0, 1):
                landed(ring1[direction, half, 3], r1.at[direction, half, 3])

        def total(half):
            return (
                g[1, 2 * z + half].astype(F32)
                + r1[0, half, 3].astype(F32)
                + r1[1, half, 3].astype(F32)
            )

        t1[...] = total(other).astype(BF)
        copy(cross1, t1, x1, x_dev).start()
        u1[...] = total(x)

    slots = [(0, 4), (0, 3), (1, 3), (0, 2), (1, 2), (0, 1), (1, 1), (0, 0)]
    slot_of = {pair: i for i, pair in enumerate(slots)}
    slot_of[1, 4] = 0

    def cross0_start():
        for i, (direction, distance) in enumerate(slots):
            copy(
                cross0[i], g.at[0, 2 * z_of(direction, distance) + other], xb.at[i], x_dev
            ).start()

    def cross0_add(i):
        landed(cross0[i], xb.at[i])
        direction, distance = slots[i]
        add(xb.at[i], g.at[0, 2 * z_of(direction, distance) + x])

    def ring0_step(k):
        for i in {0: (0,), 1: (1, 2), 2: (3, 4), 3: (5, 6)}[k]:
            cross0_add(i)
        for direction, half, first in chains(k):
            part = xb.at[slot_of[direction, 4 - k], pl.ds(48 * half, 48)]
            if first:
                src = part
            else:
                src = r0.at[direction, half, k - 1]
                landed(ring0[direction, half, k - 1], src)
                add(src, part)
            copy(ring0[direction, half, k], src, r0.at[direction, half, k], z_dev[direction]).start()

    def ring0_end():
        cross0_add(7)
        for half in (0, 1):
            rows = pl.ds(48 * half, 48)
            for direction in (0, 1):
                landed(ring0[direction, half, 3], r0.at[direction, half, 3])
            u0[rows] = (
                xb[7, rows].astype(F32) + r0[0, half, 3].astype(F32) + r0[1, half, 3].astype(F32)
            )

    y_sum = {j: message(ys.at[0]) for j in (1, 2, 3)}

    def y_reduce():
        landed(cross1, x1)
        u1[...] = u1[...] + x1[...].astype(F32)
        for p in range(4):
            ys[p, 0:16] = u0[16 * p:16 * p + 16].astype(BF)
            ys[p, 16:32] = u1[16 * p:16 * p + 16].astype(BF)
            source = u0 if p < 2 else u1
            first = 64 + 16 * (p % 2)
            ys[p, 32:48] = source[first:first + 16].astype(BF)
        for j in (1, 2, 3):
            copy(y_sum[j], ys.at[lax.rem(y + j, 4)], yr.at[j - 1], y_dev[j]).start()
        for j in (1, 2, 3):
            landed(y_sum[j], yr.at[j - 1])

    in_row = mult(64 * s_own + 16 * y, 16)
    out_head = y // 2
    out_row = mult(32 * s_own + 16 * lax.rem(y, 2), 16)

    def renorm():
        in_piece = pl.ds(mult(16 * y, 16), 16)
        out_piece = pl.ds(mult(64 + 16 * lax.rem(y, 2), 16), 16)
        total = jnp.concatenate(
            [u0[in_piece], u1[in_piece], jnp.where(y < 2, u0[out_piece], u1[out_piece])], axis=0
        )
        for j in range(3):
            total = total + yr[j].astype(F32)
        for h in (0, 1):
            old = wi[h, pl.ds(in_row, 16)].astype(F32)
            moved = old + total[16 * h:16 * h + 16] * FACTOR
            old_norm = jnp.sqrt(jnp.sum(old * old, axis=1, keepdims=True))
            new_norm = jnp.sqrt(jnp.sum(moved * moved, axis=1, keepdims=True))
            mi[h, pl.ds(in_row, 16)] = (moved * (old_norm / (new_norm + EPS))).astype(BF)
        old = wo[out_head, pl.ds(out_row, 16)].astype(F32)
        mo[out_head, pl.ds(out_row, 16)] = (old + total[32:48] * FACTOR).astype(BF)

    sixteen = mi.at[0, pl.ds(0, 16)]
    y_all = {(j, i): message(sixteen) for j in (1, 2, 3) for i in range(3)}

    def y_gather():
        pieces = (
            mi.at[0, pl.ds(in_row, 16)],
            mi.at[1, pl.ds(in_row, 16)],
            mo.at[out_head, pl.ds(out_row, 16)],
        )
        for j in (1, 2, 3):
            for i, piece in enumerate(pieces):
                copy(y_all[j, i], piece, piece, y_dev[j]).start()
        for j in (1, 2, 3):
            yy = lax.rem(y - j + 4, 4)
            row = mult(64 * s_own + 16 * yy, 16)
            landed(y_all[j, 0], mi.at[0, pl.ds(row, 16)])
            landed(y_all[j, 1], mi.at[1, pl.ds(row, 16)])
            row = mult(32 * s_own + 16 * lax.rem(yy, 2), 16)
            landed(y_all[j, 2], mo.at[yy // 2, pl.ds(row, 16)])

    def chunk(h, zz, part=None, xx=None):
        rows = 128 if h == 1 else 64
        first = 128 * zz + (64 * (x if xx is None else xx) if h == 0 or xx is not None else 0)
        if xx is not None:
            rows = 64
        n_in, f_in = rows, first
        n_out, f_out = rows // 2, first // 2
        if part is not None:
            n_in, n_out = n_in // 2, n_out // 2
            f_in = f_in + part * n_in
            f_out = f_out + part * n_out
        return (
            mi.at[h, pl.ds(mult(f_in, 16), n_in)],
            mo.at[h, pl.ds(mult(f_out, 16), n_out)],
        )

    def pair_ids(h, part=None, xx=None):
        return tuple(message(ref) for ref in chunk(h, 0, part, xx))

    def push(ids, refs, device):
        for index, ref in zip(ids, refs):
            copy(index, ref, ref, device).start()

    def pushed(ids, refs):
        for index, ref in zip(ids, refs):
            landed(index, ref)

    gather = {
        (h, j, d): pair_ids(h, d if j == 4 else None)
        for h in (0, 1) for j in (1, 2, 3, 4) for d in (0, 1)
    }
    share0 = [pair_ids(0) for _ in range(8)]
    share1 = pair_ids(1, None, x)

    def gather_send(h, j):
        for d in (0, 1):
            part = d if j == 4 else None
            push(gather[h, j, d], chunk(h, z_of(1 - d, j - 1), part), z_dev[d])

    def gather_wait(h, j):
        for d in (0, 1):
            part = d if j == 4 else None
            pushed(gather[h, j, d], chunk(h, z_of(1 - d, j), part))

    share_order = [(0, 0)] + [(d, j) for j in (1, 2, 3) for d in (0, 1)] + [(0, 4)]

    def share_send(j):
        for i, (d, jj) in enumerate(share_order):
            if jj == j:
                push(share0[i], chunk(0, z_of(1 - d, j)), x_dev)

    def share_wait():
        for i, (d, j) in enumerate(share_order):
            pushed(share0[i], chunk(0, z_of(1 - d, j), None, other))

    row = lax.broadcasted_iota(jnp.int32, (256, 256), 0)
    col = lax.broadcasted_iota(jnp.int32, (256, 256), 1)
    far_off = jnp.where(c < 2, 1e30, 0.0).astype(F32)
    near_off = jnp.where(c < 1, 1e30, 0.0).astype(F32)

    attended_heads = set()
    applied_heads = set()

    def attention(a, rb):
        ac = pl.ds(a * ADIM, ADIM)
        window = pl.ds(rb * 256, 1280)
        scores = nt(q[pl.ds(rb * 256, 256), ac], kv[0, window, ac])
        offs = (far_off, far_off, near_off, near_off, None, None)[rb:rb + 5]
        blocks = [scores[:, 256 * b:256 * b + 256] for b in range(5)]
        blocks[0] = jnp.where(col > row, blocks[0], -1e30)
        blocks[4] = jnp.where(col <= row, blocks[4], -1e30)
        top = None
        for block, off in zip(blocks, offs):
            peak = jnp.max(block, axis=1, keepdims=True)
            if off is not None:
                peak = peak - off
            top = peak if top is None else jnp.maximum(top, peak)
        base = top * SCALE
        weights = []
        for block, off in zip(blocks, offs):
            weights.append(jnp.exp2(block * SCALE - (base if off is None else base + off)))
        total = sum(jnp.sum(w, axis=1, keepdims=True) for w in weights)
        probs = jnp.concatenate([w.astype(BF) for w in weights], axis=1)
        mixed = nn(probs, kv[1, window, ac])
        rows = pl.ds(rb * 256, 256)
        if a // 5 in applied_heads:
            out[rows, ac] = (att[rows, ac] + mixed / total).astype(BF)
        else:
            att[rows, ac] = mixed / total
        attended_heads.add(a)

    def attend(strand):
        for a in (2 * strand, 2 * strand + 1):
            for rb in (0, 1):
                attention(a, rb)

    def apply(h):
        hc = pl.ds(h * HD, HD)
        queries = q[:, hc]
        gate = nt(queries, mi[h, 0:FH])
        up = nt(queries, mi[h, FH:2 * FH])
        hidden = (gate * jax.nn.sigmoid(gate) * up).astype(BF)
        old = wo[h].astype(F32)
        new = mo[h].astype(F32)
        old_norm = jnp.sqrt(jnp.sum(old * old, axis=0, keepdims=True))
        new_norm = jnp.sqrt(jnp.sum(new * new, axis=0, keepdims=True))
        applied = nn(hidden, mo[h]) * (old_norm / (new_norm + EPS))
        for a in range(5 * h, 5 * h + 5):
            ac = pl.ds(a * ADIM, ADIM)
            part = applied[:, (a - 5 * h) * ADIM:(a - 5 * h + 1) * ADIM]
            if a in attended_heads:
                out[:, ac] = (att[:, ac] + part).astype(BF)
            else:
                att[:, ac] = part
        applied_heads.add(h)

    plus_start(0)
    minus_start(3)
    plus_start(1, rest=False)
    locals_[0].wait()
    locals_[1].wait()
    locals_[2].wait()
    gradients(0)
    cross0_start()
    plus_start(1, last=False)
    minus_start(4)
    gradients(1)
    ring1_step(0)
    ring1_step(1)
    plus_relay_near(0)
    plus_relay_near(1)
    plus_forward(0, (1, 2, 3))
    minus_second(3)
    ring1_step(2)
    ring1_step(3)
    plus_forward(0, (0,))
    ring0_step(0)
    ring0_step(1)
    ring1_end()
    plus_start(2, rest=False)
    plus_forward(1, (3,))
    ring0_step(2)
    minus_hand(3)
    plus_relay_far(0)
    ring0_step(3)
    ring0_end()
    y_reduce()
    renorm()
    y_gather()
    gather_send(0, 1)
    push(share1, chunk(1, z, None, x), x_dev)
    share_send(0)
    plus_start(2, last=False)
    plus_relay_near(2)
    minus_third(3)
    minus_second(4)
    plus_forward(1, (0, 1, 2))
    relay(1, "c2", y == 3, pst.at[1, 1])
    relay(3, "cfar", y <= 1, far(3))
    pushed(share1, chunk(1, z, None, other))
    gather_send(1, 1)
    locals_[3].wait()
    for j in (1, 2, 3):
        gather_wait(0, j)
        gather_send(0, j + 1)
        share_send(j)
        gather_wait(1, j)
        gather_send(1, j + 1)
        if j == 1:
            relay(0, "xfar", y == 0, far(0))
        if j == 2:
            plus_relay_far(1)
            minus_cross(3)
        if j == 2:
            plus_done(0)
            attend(0)
            minus_hand(4)
            minus_third(4)
            plus_forward(2)
        if j == 3:
            minus_done(3)
            attend(3)
    gather_wait(0, 4)
    share_send(4)
    plus_done(1)
    attend(1)
    plus_relay_far(2)
    minus_cross(4)
    gather_wait(1, 4)
    apply(1)
    minus_done(4)
    attend(4)
    plus_done(2)
    attend(2)
    share_wait()
    apply(0)
    halo_sends_done()
    for index, ref in sent:
        copy(index, ref, ref, x_dev).wait_send()


def local(qkv, step_size, fast_in, fast_out):
    anywhere = pl.BlockSpec(memory_space=pl.ANY)
    vmem = pl.BlockSpec(memory_space=pltpu.VMEM)
    return pl.pallas_call(
        kernel,
        out_shape=jax.ShapeDtypeStruct((TOK, COLS), BF),
        in_specs=[anywhere, vmem, anywhere, anywhere],
        out_specs=vmem,
        scratch_shapes=[
            pltpu.VMEM((2, 3 * TOK, COLS), BF),
            pltpu.VMEM((TOK, COLS), BF),
            pltpu.VMEM((2, 2 * FH, HD), BF),
            pltpu.VMEM((2, FH, HD), BF),
            pltpu.VMEM((2, 16, 96, HD), BF),
            pltpu.VMEM((2, 2 * FH, HD), BF),
            pltpu.VMEM((2, FH, HD), BF),
            pltpu.VMEM((2, 2, 4, 96, HD), BF),
            pltpu.VMEM((2, 2, 4, 48, HD), BF),
            pltpu.VMEM((8, 96, HD), BF),
            pltpu.VMEM((96, HD), BF),
            pltpu.VMEM((96, HD), BF),
            pltpu.VMEM((96, HD), F32),
            pltpu.VMEM((96, HD), F32),
            pltpu.VMEM((4, 48, HD), BF),
            pltpu.VMEM((3, 48, HD), BF),
            pltpu.VMEM((3, 2, 2, TOK, STRAND), BF),
            pltpu.VMEM((2, 2, 2, TOK, STRAND), BF),
            pltpu.VMEM((len(VIA), 2, TOK, STRAND), BF),
            pltpu.VMEM((TOK, COLS), F32),
            pltpu.SemaphoreType.DMA((4,)),
            pltpu.SemaphoreType.DMA((MESSAGES,)),
            pltpu.SemaphoreType.DMA((MESSAGES,)),
        ],
        name="ttt_layer",
        compiler_params=pltpu.CompilerParams(
            collective_id=0, has_side_effects=True, vmem_limit_bytes=62 * 2**20
        ),
    )(qkv, step_size.T, fast_in.transpose(0, 2, 1), fast_out)


def solution(mesh):
    placed = (
        P(None, "ctx", "head"),
        P("ctx", "head"),
        P("head", None, None),
        P("head", None, None),
    )
    return jax.shard_map(
        local, mesh=mesh, in_specs=placed, out_specs=P("ctx", "head"), check_vma=False
    )
```

```python
import functools

import jax
import jax.numpy as jnp
from jax import lax
from jax.experimental import pallas as pl
from jax.experimental.pallas import tpu as pltpu
from jax.sharding import PartitionSpec as P

ADIM = 128
FH = 512
HD = 640
TOK = 512
COLS = 1280
EPS = 1e-06
FACTOR = 32768.0 ** -0.5
SCALE = 1.4426950408889634 * ADIM ** -0.5
STRAND = 256
PLUS = (0, 1, 2)
MINUS = (3, 4)
CROSS_NEAR_FIRST = {0: True, 1: False, 2: True}
CROSS_FAR_FIRST = {0: False, 1: True, 2: True}
VIA = {(1, "c2"): 0, (0, "xfar"): 1, (3, "cfar"): 2}
BF = jnp.bfloat16
F32 = jnp.float32
MESH = pl.DeviceIdType.MESH
MESSAGES = 160


def nt(a, b):
    return lax.dot_general(a, b, (((1,), (1,)), ((), ())), preferred_element_type=F32)


def nn(a, b):
    return jnp.dot(a, b, preferred_element_type=F32)


def mult(index, of):
    return pl.multiple_of(index, of)


def kernel(
    qkv, step, w_in, w_out, out,
    kv, q, raw, wi, wo, g, mi, mo, r1, r0, xb, x1, t1, u0, u1, ys, yr, pst, sst, vst, att,
    local_sem, ss, rs,
):
    c = lax.axis_index("ctx")
    head = lax.axis_index("head")
    y = lax.rem(c, 4)
    x = lax.rem(c // 4, 2)
    z = c // 8
    other = 1 - x
    s_own = 2 * z + x

    def at(zz, xx, yy):
        return (8 * lax.rem(zz + 16, 8) + 4 * xx + lax.rem(yy + 8, 4), head)

    y_dev = {j: at(z, x, y + j) for j in (-1, 1, 2, 3)}
    z_dev = (at(z + 1, x, y), at(z - 1, x, y))
    x_dev = at(z, other, y)
    next_dev = (lax.rem(c + 4, 64), head)
    prev_dev = (lax.rem(c + 60, 64), head)

    used = [0]
    sent = []

    def message(size_ref, always=True):
        index = used[0]
        used[0] += 1
        if always:
            sent.append((index, size_ref))
        return index

    def copy(index, src, dst, device):
        return pltpu.make_async_remote_copy(
            src_ref=src, dst_ref=dst, send_sem=ss.at[index], recv_sem=rs.at[index],
            device_id=device, device_id_type=MESH,
        )

    def landed(index, ref):
        copy(index, ref, ref, x_dev).wait_recv()

    barrier = pltpu.get_barrier_semaphore()
    for device in (y_dev[1], y_dev[2], y_dev[3], *z_dev, x_dev, next_dev, prev_dev):
        pl.semaphore_signal(barrier, inc=1, device_id=device, device_id_type=MESH)

    locals_ = []

    def fetch(src, dst):
        cp = pltpu.make_async_copy(src, dst, local_sem.at[len(locals_)])
        cp.start()
        locals_.append(cp)

    own_rows = pl.ds(2 * TOK, TOK)
    near_rows = pl.ds(TOK, TOK)
    far_rows = pl.ds(0, TOK)
    fetch(w_in, raw)
    fetch(qkv.at[pl.ds(1, 2)], kv.at[:, own_rows])
    fetch(w_out, wo)
    fetch(qkv.at[0], q)
    pl.semaphore_wait(barrier, 8)

    def cols(strand):
        return pl.ds(strand * STRAND, STRAND)

    def own(strand):
        return qkv.at[pl.ds(1, 2), :, cols(strand)]

    def near(strand):
        return kv.at[:, near_rows, cols(strand)]

    def far(strand):
        return kv.at[:, far_rows, cols(strand)]

    pid = {}
    for strand in PLUS:
        for name in ("near", "far", "c3", "c2", "xnear", "xfar"):
            pid[strand, name] = message(None, False)
    for strand in MINUS:
        for name in ("u1", "u2", "u3", "cfar"):
            pid[strand, name] = message(None, False)

    for strand, name in VIA:
        for leg in ("v", "r"):
            pid[strand, name + leg] = message(None, False)

    def halo(strand, name, src, dst, device):
        copy(pid[strand, name], src, dst, device).start()

    def cross(strand, name, src, dst):
        if (strand, name) not in VIA:
            halo(strand, name, src, dst, next_dev)
            return

        @pl.when(x == 0)
        def _():
            halo(strand, name, src, dst, next_dev)

        @pl.when(x == 1)
        def _():
            halo(strand, name + "v", src, vst.at[VIA[strand, name]], x_dev)

    def relay(strand, name, where, dst):
        if (strand, name) not in VIA:
            return

        @pl.when((x == 0) & where)
        def _():
            stage = vst.at[VIA[strand, name]]
            landed(pid[strand, name + "v"], stage)
            halo(strand, name + "r", stage, dst, z_dev[0])

    def crossed(strand, name, dst):
        if (strand, name) not in VIA:
            landed(pid[strand, name], dst)
            return

        @pl.when(x == 0)
        def _():
            landed(pid[strand, name + "r"], dst)

        @pl.when(x == 1)
        def _():
            landed(pid[strand, name], dst)

    def plus_start(strand, last=True, rest=True):
        if rest:
            @pl.when(y < 3)
            def _():
                halo(strand, "near", own(strand), near(strand), y_dev[1])

        if last:
            @pl.when(y == 3)
            def _():
                halo(strand, "c3", own(strand), pst.at[strand, 0],
                     next_dev if CROSS_NEAR_FIRST[strand] else y_dev[1])

    def plus_relay_near(strand):
        if CROSS_NEAR_FIRST[strand]:
            @pl.when(y == 3)
            def _():
                landed(pid[strand, "c3"], pst.at[strand, 0])
                halo(strand, "near", pst.at[strand, 0], near(strand), y_dev[1])
        else:
            @pl.when(y == 0)
            def _():
                landed(pid[strand, "c3"], pst.at[strand, 0])
                halo(strand, "xnear", pst.at[strand, 0], near(strand), next_dev)

    def plus_relay_far(strand):
        if CROSS_FAR_FIRST[strand]:
            @pl.when(y == 3)
            def _():
                crossed(strand, "c2", pst.at[strand, 1])
                halo(strand, "far", pst.at[strand, 1], far(strand), y_dev[1])
        else:
            @pl.when(y == 0)
            def _():
                landed(pid[strand, "c2"], pst.at[strand, 1])
                cross(strand, "xfar", pst.at[strand, 1], far(strand))

    def plus_forward(strand, ys_=(0, 1, 2, 3)):
        for yy in ys_:
            @pl.when(y == yy)
            def _():
                late = yy == 0 and not CROSS_NEAR_FIRST[strand]
                landed(pid[strand, "xnear" if late else "near"], near(strand))
                if yy < 3:
                    halo(strand, "far", near(strand), far(strand), y_dev[1])
                else:
                    if CROSS_FAR_FIRST[strand]:
                        cross(strand, "c2", near(strand), pst.at[strand, 1])
                    else:
                        halo(strand, "c2", near(strand), pst.at[strand, 1], y_dev[1])

    def plus_done(strand):
        if CROSS_FAR_FIRST[strand]:
            landed(pid[strand, "far"], far(strand))
        else:
            @pl.when(y == 0)
            def _():
                crossed(strand, "xfar", far(strand))

            @pl.when(y > 0)
            def _():
                landed(pid[strand, "far"], far(strand))

    def minus_start(strand):
        halo(strand, "u1", own(strand), sst.at[strand - MINUS[0], 0], y_dev[-1])

    def minus_second(strand):
        m = strand - MINUS[0]
        landed(pid[strand, "u1"], sst.at[m, 0])

        @pl.when((y == 0) | (y == 3))
        def _():
            halo(strand, "u2", sst.at[m, 0], far(strand), y_dev[-1])

        @pl.when((y == 1) | (y == 2))
        def _():
            halo(strand, "u2", sst.at[m, 0], sst.at[m, 1], y_dev[-1])

    def minus_hand(strand):
        m = strand - MINUS[0]

        @pl.when(y <= 1)
        def _():
            landed(pid[strand, "u2"], sst.at[m, 1])
            cross(strand, "cfar", sst.at[m, 1], far(strand))

    def minus_third(strand):
        m = strand - MINUS[0]

        @pl.when(y >= 2)
        def _():
            landed(pid[strand, "u2"], far(strand))
            halo(strand, "u3", far(strand), near(strand), y_dev[-1])

        @pl.when(y == 0)
        def _():
            halo(strand, "u3", sst.at[m, 1], near(strand), y_dev[-1])

    def minus_cross(strand):
        @pl.when(y == 1)
        def _():
            crossed(strand, "cfar", far(strand))
            halo(strand, "u3", far(strand), near(strand), y_dev[-1])

    def minus_done(strand):
        landed(pid[strand, "u3"], near(strand))

        @pl.when(y == 0)
        def _():
            crossed(strand, "cfar", far(strand))

    def halo_sends_done():
        def wait(condition, strand, name):
            @pl.when(condition)
            def _():
                copy(pid[strand, name], near(strand), near(strand), x_dev).wait_send()

        def done(condition, *which):
            for strand, name in which:
                if (strand, name) in VIA:
                    wait(condition & (x == 0), strand, name)
                    wait(condition & (x == 1), strand, name + "v")
                    wait(condition & (x == 0), strand, name + "r")
                else:
                    wait(y >= 0 if condition is None else condition, strand, name)

        for strand in PLUS:
            done(y == 3, (strand, "c3"), (strand, "c2"))
            if CROSS_NEAR_FIRST[strand]:
                done(None, (strand, "near"))
            else:
                done(y < 3, (strand, "near"))
                done(y == 0, (strand, "xnear"))
            if CROSS_FAR_FIRST[strand]:
                done(None, (strand, "far"))
            else:
                done(y < 3, (strand, "far"))
                done(y == 0, (strand, "xfar"))
        for strand in MINUS:
            done(None, (strand, "u1"), (strand, "u2"), (strand, "u3"))
            done(y <= 1, (strand, "cfar"))

    def gradients(h):
        hc = pl.ds(h * HD, HD)
        keys = kv[0, own_rows, hc]
        vals = kv[1, own_rows, hc]
        rate = jnp.broadcast_to(step[h:h + 1, :], (8, TOK)).T[:, 0:1]
        scaled = (rate * vals.astype(F32)).astype(BF)
        for part in range(4):
            wi[h, 256 * part:256 * part + 256] = raw[h, :, 256 * part:256 * part + 256].T
        gate = nt(wi[h, 0:FH], keys)
        up = nt(wi[h, FH:2 * FH], keys)
        back = nt(wo[h], scaled)
        sig = jax.nn.sigmoid(gate)
        act = gate * sig
        hidden = (act * up).astype(BF)
        d_gate = (back * up * sig * (1.0 + gate * (1.0 - sig))).astype(BF)
        d_up = (back * act).astype(BF)
        g_gate = nn(d_gate, keys).astype(BF)
        for s in range(8):
            g[h, s, 0:64] = g_gate[64 * s:64 * s + 64]
        g_up = nn(d_up, keys).astype(BF)
        for s in range(8):
            g[h, 8 + s, 0:64] = g_up[64 * s:64 * s + 64]
        g_out = nn(hidden, scaled).astype(BF)
        for s in range(16):
            g[h, s, 64:96] = g_out[32 * s:32 * s + 32]

    def add(dst, src):
        dst[...] = (dst[...].astype(F32) + src[...].astype(F32)).astype(BF)

    def z_of(direction, distance):
        offset = distance if direction == 0 else -distance
        return lax.rem(z + offset + 8, 8)

    def chains(k):
        for direction in (0, 1):
            for half in (direction, 1 - direction):
                start = 0 if half == direction else 1
                if k >= start:
                    yield direction, half, k == start

    ring1 = {(d, h, k): message(r1.at[0, 0, 0]) for k in range(4) for d, h, _ in chains(k)}
    ring0 = {(d, h, k): message(r0.at[0, 0, 0]) for k in range(4) for d, h, _ in chains(k)}
    cross0 = [message(xb.at[0]) for _ in range(8)]
    cross1 = message(x1)

    def ring1_step(k):
        for direction, half, first in chains(k):
            part = g.at[1, 2 * z_of(direction, 4 - k) + half]
            if first:
                src = part
            else:
                src = r1.at[direction, half, k - 1]
                landed(ring1[direction, half, k - 1], src)
                add(src, part)
            copy(ring1[direction, half, k], src, r1.at[direction, half, k], z_dev[direction]).start()

    def ring1_end():
        for direction in (0, 1):
            for half in (0, 1):
                landed(ring1[direction, half, 3], r1.at[direction, half, 3])

        def total(half):
            return (
                g[1, 2 * z + half].astype(F32)
                + r1[0, half, 3].astype(F32)
                + r1[1, half, 3].astype(F32)
            )

        t1[...] = total(other).astype(BF)
        copy(cross1, t1, x1, x_dev).start()
        u1[...] = total(x)

    slots = [(0, 4), (0, 3), (1, 3), (0, 2), (1, 2), (0, 1), (1, 1), (0, 0)]
    slot_of = {pair: i for i, pair in enumerate(slots)}
    slot_of[1, 4] = 0

    def cross0_start():
        for i, (direction, distance) in enumerate(slots):
            copy(
                cross0[i], g.at[0, 2 * z_of(direction, distance) + other], xb.at[i], x_dev
            ).start()

    def cross0_add(i):
        landed(cross0[i], xb.at[i])
        direction, distance = slots[i]
        add(xb.at[i], g.at[0, 2 * z_of(direction, distance) + x])

    def ring0_step(k):
        for i in {0: (0,), 1: (1, 2), 2: (3, 4), 3: (5, 6)}[k]:
            cross0_add(i)
        for direction, half, first in chains(k):
            part = xb.at[slot_of[direction, 4 - k], pl.ds(48 * half, 48)]
            if first:
                src = part
            else:
                src = r0.at[direction, half, k - 1]
                landed(ring0[direction, half, k - 1], src)
                add(src, part)
            copy(ring0[direction, half, k], src, r0.at[direction, half, k], z_dev[direction]).start()

    def ring0_end():
        cross0_add(7)
        for half in (0, 1):
            rows = pl.ds(48 * half, 48)
            for direction in (0, 1):
                landed(ring0[direction, half, 3], r0.at[direction, half, 3])
            u0[rows] = (
                xb[7, rows].astype(F32) + r0[0, half, 3].astype(F32) + r0[1, half, 3].astype(F32)
            )

    y_sum = {j: message(ys.at[0]) for j in (1, 2, 3)}

    def y_reduce():
        landed(cross1, x1)
        u1[...] = u1[...] + x1[...].astype(F32)
        for p in range(4):
            ys[p, 0:16] = u0[16 * p:16 * p + 16].astype(BF)
            ys[p, 16:32] = u1[16 * p:16 * p + 16].astype(BF)
            source = u0 if p < 2 else u1
            first = 64 + 16 * (p % 2)
            ys[p, 32:48] = source[first:first + 16].astype(BF)
        for j in (1, 2, 3):
            copy(y_sum[j], ys.at[lax.rem(y + j, 4)], yr.at[j - 1], y_dev[j]).start()
        for j in (1, 2, 3):
            landed(y_sum[j], yr.at[j - 1])

    in_row = mult(64 * s_own + 16 * y, 16)
    out_head = y // 2
    out_row = mult(32 * s_own + 16 * lax.rem(y, 2), 16)

    def renorm():
        in_piece = pl.ds(mult(16 * y, 16), 16)
        out_piece = pl.ds(mult(64 + 16 * lax.rem(y, 2), 16), 16)
        total = jnp.concatenate(
            [u0[in_piece], u1[in_piece], jnp.where(y < 2, u0[out_piece], u1[out_piece])], axis=0
        )
        for j in range(3):
            total = total + yr[j].astype(F32)
        for h in (0, 1):
            old = wi[h, pl.ds(in_row, 16)].astype(F32)
            moved = old + total[16 * h:16 * h + 16] * FACTOR
            old_norm = jnp.sqrt(jnp.sum(old * old, axis=1, keepdims=True))
            new_norm = jnp.sqrt(jnp.sum(moved * moved, axis=1, keepdims=True))
            mi[h, pl.ds(in_row, 16)] = (moved * (old_norm / (new_norm + EPS))).astype(BF)
        old = wo[out_head, pl.ds(out_row, 16)].astype(F32)
        mo[out_head, pl.ds(out_row, 16)] = (old + total[32:48] * FACTOR).astype(BF)

    sixteen = mi.at[0, pl.ds(0, 16)]
    y_all = {(j, i): message(sixteen) for j in (1, 2, 3) for i in range(3)}

    def y_gather():
        pieces = (
            mi.at[0, pl.ds(in_row, 16)],
            mi.at[1, pl.ds(in_row, 16)],
            mo.at[out_head, pl.ds(out_row, 16)],
        )
        for j in (1, 2, 3):
            for i, piece in enumerate(pieces):
                copy(y_all[j, i], piece, piece, y_dev[j]).start()
        for j in (1, 2, 3):
            yy = lax.rem(y - j + 4, 4)
            row = mult(64 * s_own + 16 * yy, 16)
            landed(y_all[j, 0], mi.at[0, pl.ds(row, 16)])
            landed(y_all[j, 1], mi.at[1, pl.ds(row, 16)])
            row = mult(32 * s_own + 16 * lax.rem(yy, 2), 16)
            landed(y_all[j, 2], mo.at[yy // 2, pl.ds(row, 16)])

    def chunk(h, zz, part=None, xx=None):
        rows = 128 if h == 1 else 64
        first = 128 * zz + (64 * (x if xx is None else xx) if h == 0 or xx is not None else 0)
        if xx is not None:
            rows = 64
        n_in, f_in = rows, first
        n_out, f_out = rows // 2, first // 2
        if part is not None:
            n_in, n_out = n_in // 2, n_out // 2
            f_in = f_in + part * n_in
            f_out = f_out + part * n_out
        return (
            mi.at[h, pl.ds(mult(f_in, 16), n_in)],
            mo.at[h, pl.ds(mult(f_out, 16), n_out)],
        )

    def pair_ids(h, part=None, xx=None):
        return tuple(message(ref) for ref in chunk(h, 0, part, xx))

    def push(ids, refs, device):
        for index, ref in zip(ids, refs):
            copy(index, ref, ref, device).start()

    def pushed(ids, refs):
        for index, ref in zip(ids, refs):
            landed(index, ref)

    gather = {
        (h, j, d): pair_ids(h, d if j == 4 else None)
        for h in (0, 1) for j in (1, 2, 3, 4) for d in (0, 1)
    }
    share0 = [pair_ids(0) for _ in range(8)]
    share1 = pair_ids(1, None, x)

    def gather_send(h, j):
        for d in (0, 1):
            part = d if j == 4 else None
            push(gather[h, j, d], chunk(h, z_of(1 - d, j - 1), part), z_dev[d])

    def gather_wait(h, j):
        for d in (0, 1):
            part = d if j == 4 else None
            pushed(gather[h, j, d], chunk(h, z_of(1 - d, j), part))

    share_order = [(0, 0)] + [(d, j) for j in (1, 2, 3) for d in (0, 1)] + [(0, 4)]

    def share_send(j):
        for i, (d, jj) in enumerate(share_order):
            if jj == j:
                push(share0[i], chunk(0, z_of(1 - d, j)), x_dev)

    def share_wait():
        for i, (d, j) in enumerate(share_order):
            pushed(share0[i], chunk(0, z_of(1 - d, j), None, other))

    row = lax.broadcasted_iota(jnp.int32, (256, 256), 0)
    col = lax.broadcasted_iota(jnp.int32, (256, 256), 1)
    far_off = jnp.where(c < 2, 1e30, 0.0).astype(F32)
    near_off = jnp.where(c < 1, 1e30, 0.0).astype(F32)

    attended_heads = set()
    applied_heads = set()

    def attention(a, rb):
        ac = pl.ds(a * ADIM, ADIM)
        window = pl.ds(rb * 256, 1280)
        scores = nt(q[pl.ds(rb * 256, 256), ac], kv[0, window, ac])
        offs = (far_off, far_off, near_off, near_off, None, None)[rb:rb + 5]
        blocks = [scores[:, 256 * b:256 * b + 256] for b in range(5)]
        blocks[0] = jnp.where(col > row, blocks[0], -1e30)
        blocks[4] = jnp.where(col <= row, blocks[4], -1e30)
        top = None
        for block, off in zip(blocks, offs):
            peak = jnp.max(block, axis=1, keepdims=True)
            if off is not None:
                peak = peak - off
            top = peak if top is None else jnp.maximum(top, peak)
        base = top * SCALE
        weights = []
        for block, off in zip(blocks, offs):
            weights.append(jnp.exp2(block * SCALE - (base if off is None else base + off)))
        total = sum(jnp.sum(w, axis=1, keepdims=True) for w in weights)
        probs = jnp.concatenate([w.astype(BF) for w in weights], axis=1)
        mixed = nn(probs, kv[1, window, ac])
        rows = pl.ds(rb * 256, 256)
        if a // 5 in applied_heads:
            out[rows, ac] = (att[rows, ac] + mixed / total).astype(BF)
        else:
            att[rows, ac] = mixed / total
        attended_heads.add(a)

    def attend(strand):
        for a in (2 * strand, 2 * strand + 1):
            for rb in (0, 1):
                attention(a, rb)

    def apply(h):
        hc = pl.ds(h * HD, HD)
        queries = q[:, hc]
        gate = nt(queries, mi[h, 0:FH])
        up = nt(queries, mi[h, FH:2 * FH])
        hidden = (gate * jax.nn.sigmoid(gate) * up).astype(BF)
        old = wo[h].astype(F32)
        new = mo[h].astype(F32)
        old_norm = jnp.sqrt(jnp.sum(old * old, axis=0, keepdims=True))
        new_norm = jnp.sqrt(jnp.sum(new * new, axis=0, keepdims=True))
        applied = nn(hidden, mo[h]) * (old_norm / (new_norm + EPS))
        for a in range(5 * h, 5 * h + 5):
            ac = pl.ds(a * ADIM, ADIM)
            part = applied[:, (a - 5 * h) * ADIM:(a - 5 * h + 1) * ADIM]
            if a in attended_heads:
                out[:, ac] = (att[:, ac] + part).astype(BF)
            else:
                att[:, ac] = part
        applied_heads.add(h)

    plus_start(0)
    minus_start(3)
    plus_start(1, rest=False)
    locals_[0].wait()
    locals_[1].wait()
    locals_[2].wait()
    gradients(0)
    cross0_start()
    plus_start(1, last=False)
    minus_start(4)
    gradients(1)
    ring1_step(0)
    ring1_step(1)
    plus_relay_near(0)
    plus_relay_near(1)
    plus_forward(0, (1, 2, 3))
    minus_second(3)
    ring1_step(2)
    ring1_step(3)
    plus_forward(0, (0,))
    minus_second(4)
    plus_start(2, last=False)
    ring0_step(0)
    ring0_step(1)
    ring1_end()
    plus_start(2, rest=False)
    plus_forward(1, (3,))
    ring0_step(2)
    minus_hand(3)
    plus_relay_far(0)
    ring0_step(3)
    ring0_end()
    y_reduce()
    renorm()
    y_gather()
    gather_send(0, 1)
    push(share1, chunk(1, z, None, x), x_dev)
    share_send(0)
    plus_relay_near(2)
    minus_third(3)
    plus_forward(1, (0, 1, 2))
    relay(1, "c2", y == 3, pst.at[1, 1])
    relay(3, "cfar", y <= 1, far(3))
    pushed(share1, chunk(1, z, None, other))
    gather_send(1, 1)
    locals_[3].wait()
    for j in (1, 2, 3):
        gather_wait(0, j)
        gather_send(0, j + 1)
        share_send(j)
        gather_wait(1, j)
        gather_send(1, j + 1)
        if j == 1:
            relay(0, "xfar", y == 0, far(0))
        if j == 2:
            plus_relay_far(1)
            minus_cross(3)
        if j == 2:
            plus_done(0)
            attend(0)
            minus_hand(4)
            minus_third(4)
            plus_forward(2)
        if j == 3:
            minus_done(3)
            attend(3)
    gather_wait(0, 4)
    share_send(4)
    plus_done(1)
    attend(1)
    plus_relay_far(2)
    minus_cross(4)
    gather_wait(1, 4)
    apply(1)
    minus_done(4)
    attend(4)
    share_wait()
    apply(0)
    plus_done(2)
    attend(2)
    halo_sends_done()
    for index, ref in sent:
        copy(index, ref, ref, x_dev).wait_send()


def local(qkv, step_size, fast_in, fast_out):
    anywhere = pl.BlockSpec(memory_space=pl.ANY)
    vmem = pl.BlockSpec(memory_space=pltpu.VMEM)
    return pl.pallas_call(
        kernel,
        out_shape=jax.ShapeDtypeStruct((TOK, COLS), BF),
        in_specs=[anywhere, vmem, anywhere, anywhere],
        out_specs=vmem,
        scratch_shapes=[
            pltpu.VMEM((2, 3 * TOK, COLS), BF),
            pltpu.VMEM((TOK, COLS), BF),
            pltpu.VMEM((2, HD, 2 * FH), BF),
            pltpu.VMEM((2, 2 * FH, HD), BF),
            pltpu.VMEM((2, FH, HD), BF),
            pltpu.VMEM((2, 16, 96, HD), BF),
            pltpu.VMEM((2, 2 * FH, HD), BF),
            pltpu.VMEM((2, FH, HD), BF),
            pltpu.VMEM((2, 2, 4, 96, HD), BF),
            pltpu.VMEM((2, 2, 4, 48, HD), BF),
            pltpu.VMEM((8, 96, HD), BF),
            pltpu.VMEM((96, HD), BF),
            pltpu.VMEM((96, HD), BF),
            pltpu.VMEM((96, HD), F32),
            pltpu.VMEM((96, HD), F32),
            pltpu.VMEM((4, 48, HD), BF),
            pltpu.VMEM((3, 48, HD), BF),
            pltpu.VMEM((3, 2, 2, TOK, STRAND), BF),
            pltpu.VMEM((2, 2, 2, TOK, STRAND), BF),
            pltpu.VMEM((len(VIA), 2, TOK, STRAND), BF),
            pltpu.VMEM((TOK, COLS), F32),
            pltpu.SemaphoreType.DMA((4,)),
            pltpu.SemaphoreType.DMA((MESSAGES,)),
            pltpu.SemaphoreType.DMA((MESSAGES,)),
        ],
        name="ttt_layer",
        compiler_params=pltpu.CompilerParams(
            collective_id=0, has_side_effects=True, vmem_limit_bytes=62 * 2**20
        ),
    )(qkv, step_size.T, fast_in, fast_out)


def solution(mesh):
    placed = (
        P(None, "ctx", "head"),
        P("ctx", "head"),
        P("head", None, None),
        P("head", None, None),
    )
    return jax.shard_map(
        local, mesh=mesh, in_specs=placed, out_specs=P("ctx", "head"), check_vma=False
    )
```

```python
import functools

import jax
import jax.numpy as jnp
from jax import lax
from jax.experimental import pallas as pl
from jax.experimental.pallas import tpu as pltpu
from jax.sharding import PartitionSpec as P

ADIM = 128
FH = 512
HD = 640
TOK = 512
COLS = 1280
EPS = 1e-06
FACTOR = 32768.0 ** -0.5
SCALE = 1.4426950408889634 * ADIM ** -0.5
STRAND = 256
PLUS = (0, 1, 2)
MINUS = (3, 4)
CROSS_NEAR_FIRST = {0: True, 1: False, 2: True}
CROSS_FAR_FIRST = {0: False, 1: True, 2: True}
VIA = {(1, "c2"): 0, (0, "xfar"): 1, (3, "cfar"): 2}
BF = jnp.bfloat16
F32 = jnp.float32
MESH = pl.DeviceIdType.MESH
MESSAGES = 160


def nt(a, b):
    return lax.dot_general(a, b, (((1,), (1,)), ((), ())), preferred_element_type=F32)


def nn(a, b):
    return jnp.dot(a, b, preferred_element_type=F32)


def mult(index, of):
    return pl.multiple_of(index, of)


def kernel(
    qkv, step, w_in, w_out, out,
    kv, q, raw, wi, wo, g, mi, mo, r1, r0, xb, x1, t1, u0, u1, ys, yr, pst, sst, vst, att,
    local_sem, ss, rs,
):
    c = lax.axis_index("ctx")
    head = lax.axis_index("head")
    y = lax.rem(c, 4)
    x = lax.rem(c // 4, 2)
    z = c // 8
    other = 1 - x
    s_own = 2 * z + x

    def at(zz, xx, yy):
        return (8 * lax.rem(zz + 16, 8) + 4 * xx + lax.rem(yy + 8, 4), head)

    y_dev = {j: at(z, x, y + j) for j in (-1, 1, 2, 3)}
    z_dev = (at(z + 1, x, y), at(z - 1, x, y))
    x_dev = at(z, other, y)
    next_dev = (lax.rem(c + 4, 64), head)
    prev_dev = (lax.rem(c + 60, 64), head)

    used = [0]
    sent = []

    def message(size_ref, always=True):
        index = used[0]
        used[0] += 1
        if always:
            sent.append((index, size_ref))
        return index

    def copy(index, src, dst, device):
        return pltpu.make_async_remote_copy(
            src_ref=src, dst_ref=dst, send_sem=ss.at[index], recv_sem=rs.at[index],
            device_id=device, device_id_type=MESH,
        )

    def landed(index, ref):
        copy(index, ref, ref, x_dev).wait_recv()

    barrier = pltpu.get_barrier_semaphore()
    for device in (y_dev[1], y_dev[2], y_dev[3], *z_dev, x_dev, next_dev, prev_dev):
        pl.semaphore_signal(barrier, inc=1, device_id=device, device_id_type=MESH)

    locals_ = []

    def fetch(src, dst):
        cp = pltpu.make_async_copy(src, dst, local_sem.at[len(locals_)])
        cp.start()
        locals_.append(cp)

    own_rows = pl.ds(2 * TOK, TOK)
    near_rows = pl.ds(TOK, TOK)
    far_rows = pl.ds(0, TOK)
    fetch(w_in, raw)
    fetch(qkv.at[pl.ds(1, 2)], kv.at[:, own_rows])
    fetch(w_out, wo)
    fetch(qkv.at[0], q)
    pl.semaphore_wait(barrier, 8)

    def cols(strand):
        return pl.ds(strand * STRAND, STRAND)

    def own(strand):
        return qkv.at[pl.ds(1, 2), :, cols(strand)]

    def near(strand):
        return kv.at[:, near_rows, cols(strand)]

    def far(strand):
        return kv.at[:, far_rows, cols(strand)]

    pid = {}
    for strand in PLUS:
        for name in ("near", "far", "c3", "c2", "xnear", "xfar"):
            pid[strand, name] = message(None, False)
    for strand in MINUS:
        for name in ("u1", "u2", "u3", "cfar"):
            pid[strand, name] = message(None, False)

    for strand, name in VIA:
        for leg in ("v", "r"):
            pid[strand, name + leg] = message(None, False)

    def halo(strand, name, src, dst, device):
        copy(pid[strand, name], src, dst, device).start()

    def cross(strand, name, src, dst):
        if (strand, name) not in VIA:
            halo(strand, name, src, dst, next_dev)
            return

        @pl.when(x == 0)
        def _():
            halo(strand, name, src, dst, next_dev)

        @pl.when(x == 1)
        def _():
            halo(strand, name + "v", src, vst.at[VIA[strand, name]], x_dev)

    def relay(strand, name, where, dst):
        if (strand, name) not in VIA:
            return

        @pl.when((x == 0) & where)
        def _():
            stage = vst.at[VIA[strand, name]]
            landed(pid[strand, name + "v"], stage)
            halo(strand, name + "r", stage, dst, z_dev[0])

    def crossed(strand, name, dst):
        if (strand, name) not in VIA:
            landed(pid[strand, name], dst)
            return

        @pl.when(x == 0)
        def _():
            landed(pid[strand, name + "r"], dst)

        @pl.when(x == 1)
        def _():
            landed(pid[strand, name], dst)

    def plus_start(strand, last=True, rest=True):
        if rest:
            @pl.when(y < 3)
            def _():
                halo(strand, "near", own(strand), near(strand), y_dev[1])

        if last:
            @pl.when(y == 3)
            def _():
                halo(strand, "c3", own(strand), pst.at[strand, 0],
                     next_dev if CROSS_NEAR_FIRST[strand] else y_dev[1])

    def plus_relay_near(strand):
        if CROSS_NEAR_FIRST[strand]:
            @pl.when(y == 3)
            def _():
                landed(pid[strand, "c3"], pst.at[strand, 0])
                halo(strand, "near", pst.at[strand, 0], near(strand), y_dev[1])
        else:
            @pl.when(y == 0)
            def _():
                landed(pid[strand, "c3"], pst.at[strand, 0])
                halo(strand, "xnear", pst.at[strand, 0], near(strand), next_dev)

    def plus_relay_far(strand):
        if CROSS_FAR_FIRST[strand]:
            @pl.when(y == 3)
            def _():
                crossed(strand, "c2", pst.at[strand, 1])
                halo(strand, "far", pst.at[strand, 1], far(strand), y_dev[1])
        else:
            @pl.when(y == 0)
            def _():
                landed(pid[strand, "c2"], pst.at[strand, 1])
                cross(strand, "xfar", pst.at[strand, 1], far(strand))

    def plus_forward(strand, ys_=(0, 1, 2, 3)):
        for yy in ys_:
            @pl.when(y == yy)
            def _():
                late = yy == 0 and not CROSS_NEAR_FIRST[strand]
                landed(pid[strand, "xnear" if late else "near"], near(strand))
                if yy < 3:
                    halo(strand, "far", near(strand), far(strand), y_dev[1])
                else:
                    if CROSS_FAR_FIRST[strand]:
                        cross(strand, "c2", near(strand), pst.at[strand, 1])
                    else:
                        halo(strand, "c2", near(strand), pst.at[strand, 1], y_dev[1])

    def plus_done(strand):
        if CROSS_FAR_FIRST[strand]:
            landed(pid[strand, "far"], far(strand))
        else:
            @pl.when(y == 0)
            def _():
                crossed(strand, "xfar", far(strand))

            @pl.when(y > 0)
            def _():
                landed(pid[strand, "far"], far(strand))

    def minus_start(strand):
        halo(strand, "u1", own(strand), sst.at[strand - MINUS[0], 0], y_dev[-1])

    def minus_second(strand):
        m = strand - MINUS[0]
        landed(pid[strand, "u1"], sst.at[m, 0])

        @pl.when((y == 0) | (y == 3))
        def _():
            halo(strand, "u2", sst.at[m, 0], far(strand), y_dev[-1])

        @pl.when((y == 1) | (y == 2))
        def _():
            halo(strand, "u2", sst.at[m, 0], sst.at[m, 1], y_dev[-1])

    def minus_hand(strand):
        m = strand - MINUS[0]

        @pl.when(y <= 1)
        def _():
            landed(pid[strand, "u2"], sst.at[m, 1])
            cross(strand, "cfar", sst.at[m, 1], far(strand))

    def minus_third(strand):
        m = strand - MINUS[0]

        @pl.when(y >= 2)
        def _():
            landed(pid[strand, "u2"], far(strand))
            halo(strand, "u3", far(strand), near(strand), y_dev[-1])

        @pl.when(y == 0)
        def _():
            halo(strand, "u3", sst.at[m, 1], near(strand), y_dev[-1])

    def minus_cross(strand):
        @pl.when(y == 1)
        def _():
            crossed(strand, "cfar", far(strand))
            halo(strand, "u3", far(strand), near(strand), y_dev[-1])

    def minus_done(strand):
        landed(pid[strand, "u3"], near(strand))

        @pl.when(y == 0)
        def _():
            crossed(strand, "cfar", far(strand))

    def halo_sends_done():
        def wait(condition, strand, name):
            @pl.when(condition)
            def _():
                copy(pid[strand, name], near(strand), near(strand), x_dev).wait_send()

        def done(condition, *which):
            for strand, name in which:
                if (strand, name) in VIA:
                    wait(condition & (x == 0), strand, name)
                    wait(condition & (x == 1), strand, name + "v")
                    wait(condition & (x == 0), strand, name + "r")
                else:
                    wait(y >= 0 if condition is None else condition, strand, name)

        for strand in PLUS:
            done(y == 3, (strand, "c3"), (strand, "c2"))
            if CROSS_NEAR_FIRST[strand]:
                done(None, (strand, "near"))
            else:
                done(y < 3, (strand, "near"))
                done(y == 0, (strand, "xnear"))
            if CROSS_FAR_FIRST[strand]:
                done(None, (strand, "far"))
            else:
                done(y < 3, (strand, "far"))
                done(y == 0, (strand, "xfar"))
        for strand in MINUS:
            done(None, (strand, "u1"), (strand, "u2"), (strand, "u3"))
            done(y <= 1, (strand, "cfar"))

    def gradients(h):
        hc = pl.ds(h * HD, HD)
        keys = kv[0, own_rows, hc]
        vals = kv[1, own_rows, hc]
        rate = jnp.broadcast_to(step[h:h + 1, :], (8, TOK)).T[:, 0:1]
        scaled = (rate * vals.astype(F32)).astype(BF)
        for part in range(4):
            wi[h, 256 * part:256 * part + 256] = raw[h, :, 256 * part:256 * part + 256].T
        gate = nt(wi[h, 0:FH], keys)
        up = nt(wi[h, FH:2 * FH], keys)
        back = nt(wo[h], scaled)
        sig = jax.nn.sigmoid(gate)
        act = gate * sig
        hidden = (act * up).astype(BF)
        d_gate = (back * up * sig * (1.0 + gate * (1.0 - sig))).astype(BF)
        d_up = (back * act).astype(BF)
        g_gate = nn(d_gate, keys).astype(BF)
        for s in range(8):
            g[h, s, 0:64] = g_gate[64 * s:64 * s + 64]
        g_up = nn(d_up, keys).astype(BF)
        for s in range(8):
            g[h, 8 + s, 0:64] = g_up[64 * s:64 * s + 64]
        g_out = nn(hidden, scaled).astype(BF)
        for s in range(16):
            g[h, s, 64:96] = g_out[32 * s:32 * s + 32]

    def add(dst, src):
        dst[...] = (dst[...].astype(F32) + src[...].astype(F32)).astype(BF)

    def z_of(direction, distance):
        offset = distance if direction == 0 else -distance
        return lax.rem(z + offset + 8, 8)

    def chains(k):
        for direction in (0, 1):
            for half in (direction, 1 - direction):
                start = 0 if half == direction else 1
                if k >= start:
                    yield direction, half, k == start

    ring1 = {(d, h, k): message(r1.at[0, 0, 0]) for k in range(4) for d, h, _ in chains(k)}
    ring0 = {(d, h, k): message(r0.at[0, 0, 0]) for k in range(4) for d, h, _ in chains(k)}
    cross0 = [message(xb.at[0]) for _ in range(8)]
    cross1 = message(x1)

    def ring1_step(k):
        for direction, half, first in chains(k):
            part = g.at[1, 2 * z_of(direction, 4 - k) + half]
            if first:
                src = part
            else:
                src = r1.at[direction, half, k - 1]
                landed(ring1[direction, half, k - 1], src)
                add(src, part)
            copy(ring1[direction, half, k], src, r1.at[direction, half, k], z_dev[direction]).start()

    def ring1_end():
        for direction in (0, 1):
            for half in (0, 1):
                landed(ring1[direction, half, 3], r1.at[direction, half, 3])

        def total(half):
            return (
                g[1, 2 * z + half].astype(F32)
                + r1[0, half, 3].astype(F32)
                + r1[1, half, 3].astype(F32)
            )

        t1[...] = total(other).astype(BF)
        copy(cross1, t1, x1, x_dev).start()
        u1[...] = total(x)

    slots = [(0, 4), (0, 3), (1, 3), (0, 2), (1, 2), (0, 1), (1, 1), (0, 0)]
    slot_of = {pair: i for i, pair in enumerate(slots)}
    slot_of[1, 4] = 0

    def cross0_start():
        for i, (direction, distance) in enumerate(slots):
            copy(
                cross0[i], g.at[0, 2 * z_of(direction, distance) + other], xb.at[i], x_dev
            ).start()

    def cross0_add(i):
        landed(cross0[i], xb.at[i])
        direction, distance = slots[i]
        add(xb.at[i], g.at[0, 2 * z_of(direction, distance) + x])

    def ring0_step(k):
        for i in {0: (0,), 1: (1, 2), 2: (3, 4), 3: (5, 6)}[k]:
            cross0_add(i)
        for direction, half, first in chains(k):
            part = xb.at[slot_of[direction, 4 - k], pl.ds(48 * half, 48)]
            if first:
                src = part
            else:
                src = r0.at[direction, half, k - 1]
                landed(ring0[direction, half, k - 1], src)
                add(src, part)
            copy(ring0[direction, half, k], src, r0.at[direction, half, k], z_dev[direction]).start()

    def ring0_end():
        cross0_add(7)
        for half in (0, 1):
            rows = pl.ds(48 * half, 48)
            for direction in (0, 1):
                landed(ring0[direction, half, 3], r0.at[direction, half, 3])
            u0[rows] = (
                xb[7, rows].astype(F32) + r0[0, half, 3].astype(F32) + r0[1, half, 3].astype(F32)
            )

    y_sum = {j: message(ys.at[0]) for j in (1, 2, 3)}

    def y_reduce():
        landed(cross1, x1)
        u1[...] = u1[...] + x1[...].astype(F32)
        for p in range(4):
            ys[p, 0:16] = u0[16 * p:16 * p + 16].astype(BF)
            ys[p, 16:32] = u1[16 * p:16 * p + 16].astype(BF)
            source = u0 if p < 2 else u1
            first = 64 + 16 * (p % 2)
            ys[p, 32:48] = source[first:first + 16].astype(BF)
        for j in (1, 2, 3):
            copy(y_sum[j], ys.at[lax.rem(y + j, 4)], yr.at[j - 1], y_dev[j]).start()
        for j in (1, 2, 3):
            landed(y_sum[j], yr.at[j - 1])

    in_row = mult(64 * s_own + 16 * y, 16)
    out_head = y // 2
    out_row = mult(32 * s_own + 16 * lax.rem(y, 2), 16)

    def renorm():
        in_piece = pl.ds(mult(16 * y, 16), 16)
        out_piece = pl.ds(mult(64 + 16 * lax.rem(y, 2), 16), 16)
        total = jnp.concatenate(
            [u0[in_piece], u1[in_piece], jnp.where(y < 2, u0[out_piece], u1[out_piece])], axis=0
        )
        for j in range(3):
            total = total + yr[j].astype(F32)
        for h in (0, 1):
            old = wi[h, pl.ds(in_row, 16)].astype(F32)
            moved = old + total[16 * h:16 * h + 16] * FACTOR
            old_norm = jnp.sqrt(jnp.sum(old * old, axis=1, keepdims=True))
            new_norm = jnp.sqrt(jnp.sum(moved * moved, axis=1, keepdims=True))
            mi[h, pl.ds(in_row, 16)] = (moved * (old_norm / (new_norm + EPS))).astype(BF)
        old = wo[out_head, pl.ds(out_row, 16)].astype(F32)
        mo[out_head, pl.ds(out_row, 16)] = (old + total[32:48] * FACTOR).astype(BF)

    sixteen = mi.at[0, pl.ds(0, 16)]
    y_all = {(j, i): message(sixteen) for j in (1, 2, 3) for i in range(3)}

    def y_gather():
        pieces = (
            mi.at[0, pl.ds(in_row, 16)],
            mi.at[1, pl.ds(in_row, 16)],
            mo.at[out_head, pl.ds(out_row, 16)],
        )
        for j in (1, 2, 3):
            for i, piece in enumerate(pieces):
                copy(y_all[j, i], piece, piece, y_dev[j]).start()
        for j in (1, 2, 3):
            yy = lax.rem(y - j + 4, 4)
            row = mult(64 * s_own + 16 * yy, 16)
            landed(y_all[j, 0], mi.at[0, pl.ds(row, 16)])
            landed(y_all[j, 1], mi.at[1, pl.ds(row, 16)])
            row = mult(32 * s_own + 16 * lax.rem(yy, 2), 16)
            landed(y_all[j, 2], mo.at[yy // 2, pl.ds(row, 16)])

    def chunk(h, zz, part=None, xx=None):
        rows = 128 if h == 1 else 64
        first = 128 * zz + (64 * (x if xx is None else xx) if h == 0 or xx is not None else 0)
        if xx is not None:
            rows = 64
        n_in, f_in = rows, first
        n_out, f_out = rows // 2, first // 2
        if part is not None:
            n_in, n_out = n_in // 2, n_out // 2
            f_in = f_in + part * n_in
            f_out = f_out + part * n_out
        return (
            mi.at[h, pl.ds(mult(f_in, 16), n_in)],
            mo.at[h, pl.ds(mult(f_out, 16), n_out)],
        )

    def pair_ids(h, part=None, xx=None):
        return tuple(message(ref) for ref in chunk(h, 0, part, xx))

    def push(ids, refs, device):
        for index, ref in zip(ids, refs):
            copy(index, ref, ref, device).start()

    def pushed(ids, refs):
        for index, ref in zip(ids, refs):
            landed(index, ref)

    gather = {
        (h, j, d): pair_ids(h)
        for h in (0, 1) for j in (1, 2, 3, 4) for d in (0, 1) if (j, d) != (4, 0)
    }
    share0 = [pair_ids(0) for _ in range(8)]
    share1 = pair_ids(1, None, x)

    def gather_send(h, j):
        for d in (0, 1) if j < 4 else (1,):
            push(gather[h, j, d], chunk(h, z_of(1 - d, j - 1)), z_dev[d])

    def gather_wait(h, j):
        for d in (0, 1) if j < 4 else (1,):
            pushed(gather[h, j, d], chunk(h, z_of(1 - d, j)))

    share_order = [(0, 0)] + [(d, j) for j in (1, 2, 3) for d in (0, 1)] + [(0, 4)]

    def share_send(j):
        for i, (d, jj) in enumerate(share_order):
            if jj == j:
                push(share0[i], chunk(0, z_of(1 - d, j)), x_dev)

    def share_wait():
        for i, (d, j) in enumerate(share_order):
            pushed(share0[i], chunk(0, z_of(1 - d, j), None, other))

    row = lax.broadcasted_iota(jnp.int32, (256, 256), 0)
    col = lax.broadcasted_iota(jnp.int32, (256, 256), 1)
    far_off = jnp.where(c < 2, 1e30, 0.0).astype(F32)
    near_off = jnp.where(c < 1, 1e30, 0.0).astype(F32)

    attended_heads = set()
    applied_heads = set()

    def attention(a, rb):
        ac = pl.ds(a * ADIM, ADIM)
        window = pl.ds(rb * 256, 1280)
        scores = nt(q[pl.ds(rb * 256, 256), ac], kv[0, window, ac])
        offs = (far_off, far_off, near_off, near_off, None, None)[rb:rb + 5]
        blocks = [scores[:, 256 * b:256 * b + 256] for b in range(5)]
        blocks[0] = jnp.where(col > row, blocks[0], -1e30)
        blocks[4] = jnp.where(col <= row, blocks[4], -1e30)
        top = None
        for block, off in zip(blocks, offs):
            peak = jnp.max(block, axis=1, keepdims=True)
            if off is not None:
                peak = peak - off
            top = peak if top is None else jnp.maximum(top, peak)
        base = top * SCALE
        weights = []
        for block, off in zip(blocks, offs):
            weights.append(jnp.exp2(block * SCALE - (base if off is None else base + off)))
        total = sum(jnp.sum(w, axis=1, keepdims=True) for w in weights)
        probs = jnp.concatenate([w.astype(BF) for w in weights], axis=1)
        mixed = nn(probs, kv[1, window, ac])
        rows = pl.ds(rb * 256, 256)
        if a // 5 in applied_heads:
            out[rows, ac] = (att[rows, ac] + mixed / total).astype(BF)
        else:
            att[rows, ac] = mixed / total
        attended_heads.add(a)

    def attend(strand):
        for a in (2 * strand, 2 * strand + 1):
            for rb in (0, 1):
                attention(a, rb)

    def apply(h):
        hc = pl.ds(h * HD, HD)
        queries = q[:, hc]
        gate = nt(queries, mi[h, 0:FH])
        up = nt(queries, mi[h, FH:2 * FH])
        hidden = (gate * jax.nn.sigmoid(gate) * up).astype(BF)
        old = wo[h].astype(F32)
        new = mo[h].astype(F32)
        old_norm = jnp.sqrt(jnp.sum(old * old, axis=0, keepdims=True))
        new_norm = jnp.sqrt(jnp.sum(new * new, axis=0, keepdims=True))
        applied = nn(hidden, mo[h]) * (old_norm / (new_norm + EPS))
        for a in range(5 * h, 5 * h + 5):
            ac = pl.ds(a * ADIM, ADIM)
            part = applied[:, (a - 5 * h) * ADIM:(a - 5 * h + 1) * ADIM]
            if a in attended_heads:
                out[:, ac] = (att[:, ac] + part).astype(BF)
            else:
                att[:, ac] = part
        applied_heads.add(h)

    plus_start(0)
    minus_start(3)
    plus_start(1, rest=False)
    locals_[0].wait()
    locals_[1].wait()
    locals_[2].wait()
    gradients(0)
    cross0_start()
    plus_start(1, last=False)
    minus_start(4)
    gradients(1)
    ring1_step(0)
    ring1_step(1)
    plus_relay_near(0)
    plus_relay_near(1)
    plus_forward(0, (1, 2, 3))
    minus_second(3)
    ring1_step(2)
    ring1_step(3)
    plus_forward(0, (0,))
    minus_second(4)
    plus_start(2, last=False)
    ring0_step(0)
    ring0_step(1)
    ring1_end()
    plus_start(2, rest=False)
    plus_forward(1, (3,))
    ring0_step(2)
    minus_hand(3)
    plus_relay_far(0)
    ring0_step(3)
    ring0_end()
    y_reduce()
    renorm()
    y_gather()
    gather_send(0, 1)
    push(share1, chunk(1, z, None, x), x_dev)
    share_send(0)
    plus_relay_near(2)
    minus_third(3)
    plus_forward(1, (0, 1, 2))
    relay(1, "c2", y == 3, pst.at[1, 1])
    relay(3, "cfar", y <= 1, far(3))
    pushed(share1, chunk(1, z, None, other))
    gather_send(1, 1)
    locals_[3].wait()
    for j in (1, 2, 3):
        gather_wait(0, j)
        gather_send(0, j + 1)
        share_send(j)
        gather_wait(1, j)
        gather_send(1, j + 1)
        if j == 1:
            relay(0, "xfar", y == 0, far(0))
        if j == 2:
            plus_relay_far(1)
            minus_cross(3)
        if j == 2:
            plus_done(0)
            attend(0)
            minus_hand(4)
            minus_third(4)
            plus_forward(2)
        if j == 3:
            minus_done(3)
            attend(3)
    gather_wait(0, 4)
    share_send(4)
    plus_done(1)
    attend(1)
    plus_relay_far(2)
    minus_cross(4)
    gather_wait(1, 4)
    apply(1)
    minus_done(4)
    attend(4)
    share_wait()
    apply(0)
    plus_done(2)
    attend(2)
    halo_sends_done()
    for index, ref in sent:
        copy(index, ref, ref, x_dev).wait_send()


def local(qkv, step_size, fast_in, fast_out):
    anywhere = pl.BlockSpec(memory_space=pl.ANY)
    vmem = pl.BlockSpec(memory_space=pltpu.VMEM)
    return pl.pallas_call(
        kernel,
        out_shape=jax.ShapeDtypeStruct((TOK, COLS), BF),
        in_specs=[anywhere, vmem, anywhere, anywhere],
        out_specs=vmem,
        scratch_shapes=[
            pltpu.VMEM((2, 3 * TOK, COLS), BF),
            pltpu.VMEM((TOK, COLS), BF),
            pltpu.VMEM((2, HD, 2 * FH), BF),
            pltpu.VMEM((2, 2 * FH, HD), BF),
            pltpu.VMEM((2, FH, HD), BF),
            pltpu.VMEM((2, 16, 96, HD), BF),
            pltpu.VMEM((2, 2 * FH, HD), BF),
            pltpu.VMEM((2, FH, HD), BF),
            pltpu.VMEM((2, 2, 4, 96, HD), BF),
            pltpu.VMEM((2, 2, 4, 48, HD), BF),
            pltpu.VMEM((8, 96, HD), BF),
            pltpu.VMEM((96, HD), BF),
            pltpu.VMEM((96, HD), BF),
            pltpu.VMEM((96, HD), F32),
            pltpu.VMEM((96, HD), F32),
            pltpu.VMEM((4, 48, HD), BF),
            pltpu.VMEM((3, 48, HD), BF),
            pltpu.VMEM((3, 2, 2, TOK, STRAND), BF),
            pltpu.VMEM((2, 2, 2, TOK, STRAND), BF),
            pltpu.VMEM((len(VIA), 2, TOK, STRAND), BF),
            pltpu.VMEM((TOK, COLS), F32),
            pltpu.SemaphoreType.DMA((4,)),
            pltpu.SemaphoreType.DMA((MESSAGES,)),
            pltpu.SemaphoreType.DMA((MESSAGES,)),
        ],
        name="ttt_layer",
        compiler_params=pltpu.CompilerParams(
            collective_id=0, has_side_effects=True, vmem_limit_bytes=62 * 2**20
        ),
    )(qkv, step_size.T, fast_in, fast_out)


def solution(mesh):
    placed = (
        P(None, "ctx", "head"),
        P("ctx", "head"),
        P("head", None, None),
        P("head", None, None),
    )
    return jax.shard_map(
        local, mesh=mesh, in_specs=placed, out_specs=P("ctx", "head"), check_vma=False
    )
```
